32 devices in a mesh: seq: 16 (over z, x, core), wshard: 2 (over y).
Axes of the slice: x: 2, y: 2, z: 4, core: 2. Of those that a mesh axis runs over, the one named last changes fastest.
Arguments:
- hidden: bfloat16 [8, 2048, 1024], P('wshard', 'seq'), may hold values from -6 to 6
- segments: int32 [8, 2048], P('wshard', 'seq'), may hold values from 0 to 2, never falling along the last dimension, each value on 1 to 1536 neighbouring positions
- cotangent: bfloat16 [8, 2048, 1024], P('wshard', 'seq'), may hold values from -6 to 6
- in_weight: bfloat16 [1024, 3, 1024], P(None, None, 'wshard'), may hold values from -0.1875 to 0.1875
- out_weight: bfloat16 [1024, 1024], P('wshard'), may hold values from -0.1875 to 0.1875
- gate_weight: bfloat16 [1024, 4608], P(None, 'wshard'), may hold values from -0.1875 to 0.1875
- up_weight: bfloat16 [1024, 4608], P(None, 'wshard'), may hold values from -0.1875 to 0.1875
- down_weight: bfloat16 [4608, 1024], P('wshard'), may hold values from -0.09375 to 0.09375
- conv_weight: bfloat16 [3, 1024], P(None, 'wshard'), may hold values from -3 to 3
- norm_mix: bfloat16 [1024], P('wshard'), may hold values from 0.5 to 1.5
- norm_ffn: bfloat16 [1024], P('wshard'), may hold values from 0.5 to 1.5
Outputs:
- block_out: bfloat16 [8, 2048, 1024], P('wshard', 'seq')
- grad_hidden: float32 [8, 2048, 1024], P('wshard', 'seq')
- grad_in: float32 [1024, 3, 1024], P('seq', None, 'wshard')
- grad_out: float32 [1024, 1024], P('wshard', 'seq')
- grad_gate: float32 [1024, 4608], P('seq', 'wshard')
- grad_up: float32 [1024, 4608], P('seq', 'wshard')
- grad_down: float32 [4608, 1024], P('wshard', 'seq')
- grad_conv: float32 [3, 1024], P(None, 'wshard')
- grad_norm_mix: float32 [1024], P('wshard')
- grad_norm_ffn: float32 [1024], P('wshard')
The draws below stay inside these ranges and needn't reach their ends.
Inputs may be any that keep to these rules, and one draw needn't show every extreme that they name: `segments`: segment numbers never fall along a sequence; each document holds 1 to 1536 tokens, one exactly that many.
All inputs are finite; a program needn't handle non-finite values.
Results may differ from the reference program's by a relative error of at most 0.017.
Values may be sent and summed in bfloat16 or wider, within the bound.
No kernel may reach another device: no remote copies, remote signals or barrier semaphores. Data moves between devices by JAX's collectives and lax.ppermute only.
A program may use at most 256 MiB of HBM per device.

```python
import math
import jax
import jax.numpy as jnp
import numpy as np
from jax import lax

D = 1024
FF = 4608
LENGTH = 2048
SEQS = 8


def levels(rng, dims, cuts, smallest, largest):
    factor_of = 1.0
    for dim, shards_of in cuts:
        heights = jax.random.uniform(jax.random.fold_in(jax.random.fold_in(rng, 6), dim), (shards_of,), jnp.float32, smallest / len(cuts), largest / len(cuts))
        factor_of = factor_of * jnp.repeat(jnp.exp(heights), dims[dim] // shards_of).reshape((-1,) + (1,) * (len(dims) - 1 - dim))
    return factor_of


def split_up(number_of, total, most, lean):
    weights = [(1 << 20) // math.isqrt(grade ** lean) + 1 for grade in range(2, number_of + 1)]
    rest, holding = total - most - (number_of - 1), [1] * (number_of - 1)
    while rest > 0:
        free = [i for i in range(number_of - 1) if holding[i] < most]
        whole, budget = sum([weights[i] for i in free]), rest
        for i in free:
            extra = min(most - holding[i], max(1, budget * weights[i] // whole), rest)
            holding[i] = holding[i] + extra
            rest = rest - extra
    return np.array([most] + holding)


def ragged(own_key, number_of, total, reach, slope):
    if number_of == 2:
        one = jax.random.randint(own_key, (), max(1, total - reach), min(reach, total - 1) + 1)
        return jnp.stack([one, total - one])
    lengths = jnp.asarray(split_up(number_of, total, reach, slope), jnp.int32)
    pairs = (number_of - 1) // 2
    giver, taker = lengths[1:1 + 2 * pairs:2], lengths[2:2 + 2 * pairs:2]
    margin = jnp.minimum(giver - 1, reach - taker)
    moved = jax.random.randint(jax.random.fold_in(own_key, 1), (pairs,), 0, 1 << 20) % (margin + 1)
    lengths = lengths.at[1:1 + 2 * pairs:2].set(giver - moved).at[2:2 + 2 * pairs:2].set(taker + moved)
    return lengths[jax.random.permutation(jax.random.fold_in(own_key, 2), number_of)]


def gaussian(own_key, shape, spread, reach, shards=(), kind=jnp.bfloat16):
    values = spread * jax.random.normal(own_key, shape, jnp.float32)
    if shards:
        values = values * levels(own_key, shape, shards, -0.22, 0.18)
    return jnp.clip(values, -reach, reach).astype(kind)


def setup_inputs(seed: int = 0) -> dict:
    seeds = jax.random.split(jax.random.key(seed), 12)
    hidden = gaussian(seeds[0], (SEQS, LENGTH, D), 1.0, 6.0, ((0, 2), (1, 16)))
    segments = jax.vmap(lambda own: jnp.searchsorted(jnp.cumsum(ragged(own, max(3, LENGTH // 1024), LENGTH, 3 * LENGTH // 4, 2)), jnp.arange(LENGTH), side="right"))(jax.random.split(seeds[1], SEQS)).reshape((SEQS, LENGTH)).astype(jnp.int32)
    cotangent = gaussian(seeds[2], (SEQS, LENGTH, D), 1.0, 6.0, ((0, 2), (1, 16)))
    in_weight = gaussian(seeds[3], (D, 3, D), D ** -0.5, 0.1875, ((2, 2),))
    out_weight = gaussian(seeds[4], (D, D), D ** -0.5, 0.1875, ((0, 2),))
    gate_weight = gaussian(seeds[5], (D, FF), D ** -0.5, 0.1875, ((1, 2),))
    up_weight = gaussian(seeds[6], (D, FF), D ** -0.5, 0.1875, ((1, 2),))
    down_weight = gaussian(seeds[7], (FF, D), FF ** -0.5, 0.09375, ((0, 2),))
    conv_weight = gaussian(seeds[8], (3, D), 0.5, 3.0, ((1, 2),))
    norm_mix = jnp.clip(1.0 + 0.1 * jax.random.normal(seeds[9], (D,), jnp.float32), 0.5, 1.5).astype(jnp.bfloat16)
    norm_ffn = jnp.clip(1.0 + 0.1 * jax.random.normal(seeds[10], (D,), jnp.float32), 0.5, 1.5).astype(jnp.bfloat16)
    return dict(hidden=hidden, segments=segments, cotangent=cotangent, in_weight=in_weight, out_weight=out_weight, gate_weight=gate_weight, up_weight=up_weight, down_weight=down_weight, conv_weight=conv_weight, norm_mix=norm_mix, norm_ffn=norm_ffn)


EPS = 1e-05

@jax.custom_vjp
def low(v):
    return lax.optimization_barrier(v.astype(jnp.bfloat16)).astype(jnp.float32)

@jax.custom_vjp
def low_back(v):
    return v

def low_keep(v):
    return (low(v), None)

def low_pass(kept, grad):
    return (grad,)

def back_keep(v):
    return (v, None)

def back_low(kept, grad):
    return (low(grad),)
low.defvjp(low_keep, low_pass)
low_back.defvjp(back_keep, back_low)

def rms_norm(values, gain):
    scale = lax.rsqrt(lax.optimization_barrier(jnp.mean(values * values, axis=-1, keepdims=True)) + EPS)
    return values * scale * gain

def masked_conv(conv_in, taps, seg_ids):
    total = taps[2] * conv_in
    for offset in (1, 2):
        earlier = jnp.concatenate([jnp.zeros((offset, conv_in.shape[1]), jnp.float32), conv_in[:-offset]], axis=0)
        earlier_ids = jnp.concatenate([jnp.full((offset,), -1, jnp.int32), seg_ids[:-offset]], axis=0)
        keep = (earlier_ids == seg_ids).astype(jnp.float32)[:, None]
        total = total + taps[2 - offset] * earlier * keep
    return total

def block_forward(resid, in_weight, out_weight, gate_weight, up_weight, down_weight, conv_weight, norm_mix, norm_ffn, seg_ids):
    highest = lax.Precision.HIGHEST
    width = resid.shape[1]
    in_matrix = in_weight.reshape(width, 3 * width)
    normed_mix = low(rms_norm(resid, norm_mix))
    projected = low_back(jnp.dot(normed_mix, in_matrix, precision=highest))
    b_part = projected[:, :width]
    c_part = projected[:, width:2 * width]
    x_part = projected[:, 2 * width:]
    conv_in = low(b_part * x_part)
    mixed = low(c_part * masked_conv(conv_in, conv_weight, seg_ids))
    resid_two = resid + low_back(jnp.dot(mixed, out_weight, precision=highest))
    normed_ffn = low(rms_norm(resid_two, norm_ffn))
    gate = low_back(jnp.dot(normed_ffn, gate_weight, precision=highest))
    up_value = low_back(jnp.dot(normed_ffn, up_weight, precision=highest))
    act = low(jax.nn.silu(gate) * up_value)
    return resid_two + low_back(jnp.dot(act, down_weight, precision=highest))

def reference(hidden, segments, cotangent, in_weight, out_weight, gate_weight, up_weight, down_weight, conv_weight, norm_mix, norm_ffn):
    weights = tuple((item.astype(jnp.float32) for item in (in_weight, out_weight, gate_weight, up_weight, down_weight, conv_weight, norm_mix, norm_ffn)))

    def per_sequence(totals, inputs):
        resid, seg_ids, upstream = inputs

        def forward(state, *params):
            return block_forward(state, *params, seg_ids)
        result, pullback = jax.vjp(forward, resid.astype(jnp.float32), *weights)
        grads = pullback(upstream.astype(jnp.float32))
        totals = tuple((carried + added for carried, added in zip(totals, grads[1:])))
        return (totals, (result.astype(jnp.bfloat16), grads[0]))
    start = tuple((jnp.zeros_like(item) for item in weights))
    totals, outputs = lax.scan(per_sequence, start, (hidden, segments, cotangent))
    return (outputs[0], outputs[1], totals[0], totals[1], totals[2], totals[3], totals[4], totals[5], totals[6], totals[7])
```

```python
import jax
import jax.numpy as jnp
from jax import lax
from jax.sharding import PartitionSpec as P

EPS = 1e-05
LOW = jnp.bfloat16
F32 = jnp.float32


def over_seq(block, route):
    return lax.ppermute(block, "seq", route)


def swap_seq(block, mask):
    return over_seq(block, [(i, i ^ mask) for i in range(lax.axis_size("seq"))])


def swap_core(block):
    return swap_seq(block, 1)


def swap_pair(block):
    return lax.ppermute(block, "wshard", [(0, 1), (1, 0)])


def swap(block, link):
    return swap_pair(block) if link == "pair" else swap_seq(block, 2 * link)


def mm(left, right):
    return jnp.dot(left, right, preferred_element_type=F32)


def mm_tn(left, right):
    return lax.dot_general(left, right, (((0,), (0,)), ((), ())), preferred_element_type=F32)


def mm_nt(left, right):
    return lax.dot_general(left, right, (((1,), (1,)), ((), ())), preferred_element_type=F32)


def norm_stats(values):
    return lax.rsqrt(jnp.mean(values * values, axis=-1, keepdims=True) + EPS)


def norm_back(upstream, values, scale, gain):
    scaled = values * scale
    weighted = upstream * gain
    inner = jnp.mean(weighted * scaled, axis=-1, keepdims=True)
    return scale * (weighted - scaled * inner)


def slot_masks(order):
    masks = [0]
    for link in reversed(order):
        masks = masks + [mask ^ link for mask in masks]
    return masks


def in_slots(grad, chip, order):
    chips = lax.axis_size("seq") // 2
    blocks = grad.astype(LOW).reshape(chips, grad.shape[0] // chips, grad.shape[1])
    return jnp.stack(
        [lax.dynamic_index_in_dim(blocks, chip ^ mask, 0, False) for mask in slot_masks(order)]
    )


def halving(send, keep, order):
    terms = [keep]
    half = keep.shape[0]
    terms.append(swap(send, order[0]))
    for link in order[1:]:
        half //= 2
        going = sum(term[half : 2 * half].astype(F32) for term in terms).astype(LOW)
        terms.append(swap(going, link))
    return sum(term[0].astype(F32) for term in terms)


def scatter_seq(grad, chip, order):
    slots = in_slots(grad, chip, order)
    half = slots.shape[0] // 2
    return halving(slots[half:], slots[:half], order)


def scatter_all(mine, other, chip, order):
    return halving(in_slots(other, chip, order[1:]), in_slots(mine, chip, order[1:]), order)


def local(
    hidden,
    segments,
    cotangent,
    in_weight,
    out_weight,
    gate_weight,
    up_weight,
    down_weight,
    conv_weight,
    norm_mix,
    norm_ffn,
):
    groups, block, width = hidden.shape
    rows = groups * block
    size = lax.axis_size("seq")
    seq_index = lax.axis_index("seq")
    core = seq_index % 2
    chip = seq_index // 2
    pair = lax.axis_index("wshard")
    first_core = core == 0
    chips = size // 2
    links = [1 << bit for bit in range(chips.bit_length() - 1)]
    features = out_weight.shape[0] // 2
    units = gate_weight.shape[1] // 2

    def ordered(flag, mine, other, axis):
        return jnp.where(
            flag,
            jnp.concatenate([mine, other], axis=axis),
            jnp.concatenate([other, mine], axis=axis),
        )

    small = jnp.concatenate([conv_weight, norm_mix[None], norm_ffn[None]], axis=0)
    small_other = swap_pair(small)
    gains = ordered(pair == 0, small[3:], small_other[3:], 1).astype(F32)
    gain_mix, gain_ffn = gains[0], gains[1]

    def of_core(array, axis):
        return lax.dynamic_slice_in_dim(array, core * (array.shape[axis] // 2), array.shape[axis] // 2, axis)

    taps = jnp.concatenate([of_core(small[:3], 1), of_core(small_other[:3], 1)], axis=1).astype(F32)

    in_mine = of_core(jnp.transpose(in_weight, (1, 0, 2)), 2)
    in_other = swap_pair(in_mine)
    out_mine = of_core(out_weight, 0)
    out_other = swap_pair(out_mine)
    in_mat = jnp.concatenate(
        [part for j in range(3) for part in (in_mine[j], in_other[j])], axis=1
    )
    out_mat = jnp.concatenate([out_mine, out_other], axis=0)
    conv_width = 2 * features

    own = hidden.reshape(rows, width)
    chip_hidden = jnp.concatenate([own, swap_core(own)], axis=0)
    seg_low = segments.astype(LOW)
    seg_other = swap_core(segments)

    edge = jnp.concatenate(
        [hidden, jnp.broadcast_to(seg_low[:, :, None], (groups, block, 128))], axis=2
    )
    last, head = edge[:, block - 2 :], edge[:, :2]
    odd = range(1, size - 1, 2)
    even = range(2, size, 2)
    before = jnp.where(
        first_core,
        over_seq(last, [(i, i + 1) for i in odd]),
        over_seq(last, [(i, i + 2) for i in odd]),
    )
    after = jnp.where(
        first_core,
        over_seq(head, [(i, i - 2) for i in even]),
        over_seq(head, [(i, i - 1) for i in even]),
    )
    edges = jnp.concatenate([before, after], axis=0)
    edge_hidden = edges[:, :, :width].reshape(4 * groups, width)
    edge_segs = edges[:, :, width].astype(jnp.int32)

    resid = chip_hidden.astype(F32)
    scale_mix = norm_stats(resid)
    normed_mix = (resid * scale_mix * gain_mix).astype(LOW)
    edge_resid = edge_hidden.astype(F32)
    edge_normed = (edge_resid * norm_stats(edge_resid) * gain_mix).astype(LOW)
    projected = mm(normed_mix, in_mat)
    edge_projected = mm(edge_normed, in_mat)
    b_part = projected[:, :conv_width]
    c_part = projected[:, conv_width : 2 * conv_width]
    x_part = projected[:, 2 * conv_width :]

    def by_core(array):
        return array.reshape((2, groups, block) + array.shape[1:])

    def lead(own_lead, other_lead):
        return jnp.stack([own_lead, other_lead])

    conv_in = by_core((b_part * x_part).astype(LOW).astype(F32))
    edge_conv_in = (
        (edge_projected[: 2 * groups, :conv_width] * edge_projected[: 2 * groups, 2 * conv_width :])
        .astype(LOW)
        .astype(F32)
        .reshape(groups, 2, conv_width)
    )
    edge_c = edge_projected[2 * groups :, conv_width : 2 * conv_width]
    segs = jnp.stack([segments, seg_other])
    segs_before, segs_after = edge_segs[:groups], edge_segs[groups:]

    def with_before(values, outside):
        ahead = jnp.where(
            first_core,
            lead(outside, values[0, :, block - 2 :]),
            lead(values[1, :, block - 2 :], outside),
        )
        return jnp.concatenate([ahead, values], axis=2)

    def with_after(values, outside):
        behind = jnp.where(
            first_core, lead(values[1, :, :2], outside), lead(outside, values[0, :, :2])
        )
        return jnp.concatenate([values, behind], axis=2)

    ext = with_before(conv_in, edge_conv_in)
    segs_ext = with_before(segs, segs_before)
    keep_one = (segs_ext[:, :, 1 : 1 + block] == segs).astype(F32)[..., None]
    keep_two = (segs_ext[:, :, :block] == segs).astype(F32)[..., None]
    lag_one = keep_one * ext[:, :, 1 : 1 + block]
    lag_two = keep_two * ext[:, :, :block]
    conv_out = (taps[2] * conv_in + taps[1] * lag_one + taps[0] * lag_two).reshape(2 * rows, conv_width)
    mixed = (c_part * conv_out).astype(LOW)
    mix_part = mm(mixed, out_mat).astype(LOW)
    mix_other = swap_core(mix_part)
    mix_term = mix_part.astype(F32) + jnp.concatenate([mix_other[rows:], mix_other[:rows]], axis=0).astype(F32)
    resid_two = resid + mix_term
    scale_ffn = norm_stats(resid_two)
    normed_ffn = (resid_two * scale_ffn * gain_ffn).astype(LOW)

    def gathered(mine):
        far = swap_pair(mine)
        return far, swap_core(far)

    cot = cotangent.reshape(rows, width)
    cot_chip = jnp.concatenate([cot, swap_core(cot)], axis=0)
    cot_far = jnp.concatenate(gathered(cot), axis=0)
    normed_far = jnp.concatenate(gathered(normed_ffn[:rows]), axis=0)
    gate_mat = of_core(gate_weight, 1)
    up_mat = of_core(up_weight, 1)
    down_mat = of_core(down_weight, 0)

    def feed_forward(normed, upstream):
        gate = mm(normed, gate_mat)
        up_value = mm(normed, up_mat)
        d_act = mm_nt(upstream, down_mat)
        sigma = jax.nn.sigmoid(gate)
        silu_gate = gate * sigma
        act = (silu_gate * up_value).astype(LOW)
        d_gate = (d_act * up_value * sigma * (1.0 + gate * (1.0 - sigma))).astype(LOW)
        d_up = (d_act * silu_gate).astype(LOW)
        term = mm(act, down_mat).astype(LOW)
        d_normed = (mm_nt(d_gate, gate_mat) + mm_nt(d_up, up_mat)).astype(LOW)
        return act, d_gate, d_up, term, d_normed

    near_out = feed_forward(normed_ffn, cot_chip)
    far_out = feed_forward(normed_far, cot_far)

    def home(near, far):
        near_sum = near[:rows].astype(F32) + swap_core(near[rows:]).astype(F32)
        far_sum = (far[:rows].astype(F32) + swap_core(far[rows:]).astype(F32)).astype(LOW)
        return near_sum + swap_pair(far_sum).astype(F32)

    d_normed_ffn = home(near_out[4], far_out[4])
    block_out = (resid_two[:rows] + home(near_out[3], far_out[3])).astype(LOW)

    all_normed = jnp.concatenate([normed_ffn, normed_far], axis=0)
    all_cot = jnp.concatenate([cot_chip, cot_far], axis=0)
    act, d_gate, d_up = (jnp.concatenate([near_out[i], far_out[i]], axis=0) for i in range(3))
    part_down = scatter_seq(mm_tn(all_cot, act), chip, links)
    part_gate = scatter_seq(mm_tn(all_normed, d_gate), chip, links)
    part_up = scatter_seq(mm_tn(all_normed, d_up), chip, links)

    upstream = cot.astype(F32)
    own_two, own_scale = resid_two[:rows], scale_ffn[:rows]
    d_resid_two = upstream + norm_back(d_normed_ffn, own_two, own_scale, gain_ffn)
    grad_gain_ffn = jnp.sum(d_normed_ffn * own_two * own_scale, axis=0)
    d_resid_low = d_resid_two.astype(LOW)
    d_chip = jnp.concatenate([d_resid_low, swap_core(d_resid_low)], axis=0)
    d_head = d_resid_low.reshape(groups, block, width)[:, :2]
    d_after = jnp.where(
        first_core,
        over_seq(d_head, [(i, i - 2) for i in even]),
        over_seq(d_head, [(i, i - 1) for i in even]),
    ).reshape(2 * groups, width)
    d_mixed = mm_nt(d_chip, out_mat)
    edge_d_conv = (mm_nt(d_after, out_mat) * edge_c).reshape(groups, 2, conv_width)
    d_conv = by_core(d_mixed * c_part)
    d_c = d_mixed * conv_out
    grad_taps = jnp.stack(
        [
            jnp.sum(d_conv * lag_two, axis=(0, 1, 2)),
            jnp.sum(d_conv * lag_one, axis=(0, 1, 2)),
            jnp.sum(d_conv * conv_in, axis=(0, 1, 2)),
        ]
    )
    d_ext = with_after(d_conv, edge_d_conv)
    segs_next = with_after(segs, segs_after)
    next_one = (segs_next[:, :, 1 : 1 + block] == segs).astype(F32)[..., None]
    next_two = (segs_next[:, :, 2 : 2 + block] == segs).astype(F32)[..., None]
    d_conv_in = (
        taps[2] * d_conv
        + taps[1] * next_one * d_ext[:, :, 1 : 1 + block]
        + taps[0] * next_two * d_ext[:, :, 2 : 2 + block]
    ).reshape(2 * rows, conv_width)
    d_proj = jnp.concatenate([d_conv_in * x_part, d_c, d_conv_in * b_part], axis=1).astype(LOW)
    grad_out = mm_tn(d_chip, mixed)
    grad_in = mm_tn(normed_mix, d_proj)
    d_normed_part = mm_nt(d_proj, in_mat).astype(LOW)
    d_normed_mix = d_normed_part[:rows].astype(F32) + swap_core(d_normed_part[rows:]).astype(F32)
    own_resid, own_mix = resid[:rows], scale_mix[:rows]
    grad_hidden = (d_resid_two + norm_back(d_normed_mix, own_resid, own_mix, gain_mix)).reshape(
        groups, block, width
    )
    grad_gain_mix = jnp.sum(d_normed_mix * own_resid * own_mix, axis=0)

    halves = [grad_out] + [grad_in[:, j * conv_width : (j + 1) * conv_width] for j in range(3)]
    mixed_mine = jnp.concatenate([half[:, :features] for half in halves], axis=1)
    mixed_far = jnp.concatenate([half[:, features:] for half in halves], axis=1)
    part_mix = scatter_all(mixed_mine, mixed_far, chip, ["pair"] + links)

    part_rows = width // size

    def finish(part):
        low = part.astype(LOW).reshape(2, part_rows, -1)
        came = swap_core(lax.dynamic_index_in_dim(low, 1 - core, 0, False)).astype(F32)
        mine = lax.dynamic_index_in_dim(part.reshape(2, part_rows, -1), core, 0, False)
        return mine, came

    def wide(part):
        mine, came = finish(part)
        return ordered(first_core, mine, came, 1)

    out_down = wide(part_down).T
    out_gate = wide(part_gate)
    out_up = wide(part_up)
    mix_mine, mix_came = finish(part_mix)
    mix_parts = [
        ordered(
            first_core,
            mix_mine[:, j * features : (j + 1) * features],
            mix_came[:, j * features : (j + 1) * features],
            1,
        )
        for j in range(4)
    ]
    out_out = mix_parts[0].T
    out_in = jnp.stack(mix_parts[1:], axis=1)

    half_width = norm_mix.shape[0]
    spread = jnp.zeros((3, width), F32)
    spread = lax.dynamic_update_slice_in_dim(
        spread, grad_taps[:, :features], pair * half_width + core * features, 1
    )
    spread = lax.dynamic_update_slice_in_dim(
        spread, grad_taps[:, features:], (1 - pair) * half_width + core * features, 1
    )
    sums = lax.psum(
        jnp.concatenate([spread, grad_gain_mix[None], grad_gain_ffn[None]], axis=0), ("seq", "wshard")
    )
    sums = lax.dynamic_slice_in_dim(sums, pair * half_width, half_width, 1)
    return (
        block_out.reshape(groups, block, width),
        grad_hidden,
        out_in,
        out_out,
        out_gate,
        out_up,
        out_down,
        sums[:3],
        sums[3],
        sums[4],
    )


def solution(mesh):
    return jax.shard_map(
        local,
        mesh=mesh,
        in_specs=(
            P("wshard", "seq", None),
            P("wshard", "seq"),
            P("wshard", "seq", None),
            P(None, None, "wshard"),
            P("wshard", None),
            P(None, "wshard"),
            P(None, "wshard"),
            P("wshard", None),
            P(None, "wshard"),
            P("wshard"),
            P("wshard"),
        ),
        out_specs=(
            P("wshard", "seq", None),
            P("wshard", "seq", None),
            P("seq", None, "wshard"),
            P("wshard", "seq"),
            P("seq", "wshard"),
            P("seq", "wshard"),
            P("wshard", "seq"),
            P(None, "wshard"),
            P("wshard"),
            P("wshard"),
        ),
        check_vma=False,
    )
```

```python
import functools

import jax
import jax.numpy as jnp
from jax import lax
from jax.experimental import pallas as pl
from jax.experimental.pallas import tpu as pltpu
from jax.sharding import PartitionSpec as P

EPS = 1e-05
LOW = jnp.bfloat16
F32 = jnp.float32
TILE = 256
NT = (((1,), (1,)), ((), ()))
TN = (((0,), (0,)), ((), ()))


def over_seq(block, route):
    return lax.ppermute(block, "seq", route)


def swap_seq(block, mask):
    return over_seq(block, [(i, i ^ mask) for i in range(lax.axis_size("seq"))])


def swap_core(block):
    return swap_seq(block, 1)


def swap_pair(block):
    return lax.ppermute(block, "wshard", [(0, 1), (1, 0)])


def swap(block, link):
    return swap_pair(block) if link == "pair" else swap_seq(block, 2 * link)


def tie(value, *after):
    return lax.optimization_barrier((value,) + after)[0]


def dot(left, right):
    return jnp.dot(left, right, preferred_element_type=F32)


def dot_nt(left, right):
    return lax.dot_general(left, right, NT, preferred_element_type=F32)


def dot_tn(left, right):
    return lax.dot_general(left, right, TN, preferred_element_type=F32)


def call(body, name, grid, in_specs, out_specs, out_shape, scratch=(), scalars=1, aliases=None):
    return pl.pallas_call(
        body,
        grid_spec=pltpu.PrefetchScalarGridSpec(
            num_scalar_prefetch=scalars,
            grid=grid,
            in_specs=in_specs,
            out_specs=out_specs,
            scratch_shapes=list(scratch),
        ),
        out_shape=out_shape,
        input_output_aliases=aliases or {},
        compiler_params=pltpu.CompilerParams(vmem_limit_bytes=56 * 2**20),
        cost_estimate=pl.CostEstimate(flops=1000, bytes_accessed=1000, transcendentals=0),
        name=name,
    )


def shape(rows, cols, kind=LOW):
    return jax.ShapeDtypeStruct((rows, cols), kind)


def whole(array):
    zeros = (0,) * array.ndim
    return pl.BlockSpec(array.shape, lambda *_: zeros)


def normed(values, gain):
    wide = values.astype(F32)
    scale = lax.rsqrt(jnp.mean(wide * wide, axis=-1, keepdims=True) + EPS)
    return wide * scale * gain, scale


def piece_columns(place, j, depth):
    return pl.ds(pl.multiple_of((place ^ j) * depth, depth), depth)


def conv_forward_body(
    block,
    idx,
    x_ref,
    edge_ref,
    in_ref,
    out_ref,
    r0,
    r1,
    r2,
    r3,
    gain_ref,
    taps_ref,
    keep_ref,
    normed_ref,
    parts_ref,
    conv_in_ref,
    conv_out_ref,
    mixed_ref,
    mix_ref,
    c_edge_ref,
    nx,
    edge_in,
    acc,
):
    step = pl.program_id(0)
    place = idx[1]
    far = (r0, r1, r2, r3)
    depth = r0.shape[1]
    half = r0.shape[2]
    cols = 2 * half
    gain = gain_ref[...]

    def project(load, j):
        mine = dot(load(slice(None)), in_ref[j])
        other = None
        for p in range(4):
            term = dot(load(piece_columns(place, p, depth)), far[p][j])
            other = term if other is None else other + term
        return jnp.concatenate([mine, other], axis=1)

    @pl.when(step == 0)
    def _():
        count = edge_ref.shape[0]
        nx[:count] = normed(edge_ref[...], gain)[0].astype(LOW)

        def load(columns):
            return nx[:count, columns]

        before = count // 2
        edge_b, edge_c, edge_x = (project(load, j) for j in range(3))
        edge_in[...] = (edge_b[:before] * edge_x[:before]).astype(LOW).astype(F32)
        c_edge_ref[...] = edge_c[before:]

    nx[...] = normed(x_ref[...], gain)[0].astype(LOW)
    normed_ref[...] = nx[...]

    def load(columns):
        return nx[:, columns]

    b_part, c_part, x_part = (project(load, j) for j in range(3))
    parts_ref[:, :cols] = b_part.astype(LOW)
    parts_ref[:, cols : 2 * cols] = c_part.astype(LOW)
    parts_ref[:, 2 * cols :] = x_part.astype(LOW)
    low_in = (b_part * x_part).astype(LOW)
    conv_in_ref[...] = low_in
    conv_in = low_in.astype(F32)
    groups = x_ref.shape[0] // block
    row = lax.broadcasted_iota(jnp.int32, (block, cols), 0)
    for g in range(groups):
        span = slice(g * block, (g + 1) * block)
        here = conv_in[span]
        base = step * 2 * groups + 2 * g
        two_before = edge_in[pl.ds(base, 1), :]
        one_before = edge_in[pl.ds(base + 1, 1), :]
        lag_one = jnp.where(row == 0, one_before, pltpu.roll(here, 1, 0))
        lag_two = jnp.where(
            row == 0, two_before, jnp.where(row == 1, one_before, pltpu.roll(here, 2, 0))
        )
        conv_out = (
            taps_ref[2:3, :] * here
            + taps_ref[1:2, :] * (keep_ref[span, 0:1] * lag_one)
            + taps_ref[0:1, :] * (keep_ref[span, 1:2] * lag_two)
        )
        conv_out_ref[span, :] = conv_out.astype(LOW)
        mixed_ref[span, :] = (c_part[span] * conv_out).astype(LOW)
    mixed = mixed_ref[...]
    acc[...] = dot(mixed[:, :half], out_ref[...])
    for p in range(4):
        where = piece_columns(place, p, depth)
        acc[:, where] += dot(mixed[:, half:], far[p][3])
    mix_ref[...] = acc[...].astype(LOW)


def conv_forward(idx, x, edges, in_weight, out_weight, far, gain, taps, keeps, block):
    total, width = x.shape
    rows = TILE
    half = far[0].shape[2]
    cols = 2 * half

    def rowed(columns):
        return pl.BlockSpec((rows, columns), lambda i, s: (i, 0))

    before = edges.shape[0] // 2
    return call(
        functools.partial(conv_forward_body, block),
        "conv_forward",
        (total // rows,),
        [
            rowed(width),
            whole(edges),
            pl.BlockSpec((3, width, half), lambda i, s: (0, 0, s[0])),
            pl.BlockSpec((half, width), lambda i, s: (s[0], 0)),
            *[whole(piece) for piece in far],
            whole(gain),
            whole(taps),
            rowed(keeps.shape[1]),
        ],
        [
            rowed(width),
            rowed(3 * cols),
            rowed(cols),
            rowed(cols),
            rowed(cols),
            rowed(width),
            pl.BlockSpec((before, cols), lambda i, s: (0, 0)),
        ],
        [
            shape(total, width),
            shape(total, 3 * cols),
            shape(total, cols),
            shape(total, cols),
            shape(total, cols),
            shape(total, width),
            shape(before, cols, F32),
        ],
        [
            pltpu.VMEM((rows, width), LOW),
            pltpu.VMEM((before, cols), F32),
            pltpu.VMEM((rows, width), F32),
        ],
    )(idx, x, edges, in_weight, out_weight, *far, gain, taps, keeps)


def second_norm_body(x_ref, mine_ref, came_ref, gain_ref, low_ref, *resid_ref):
    two = x_ref[...].astype(F32) + (mine_ref[...].astype(F32) + came_ref[...].astype(F32))
    low_ref[...] = normed(two, gain_ref[...])[0].astype(LOW)
    for ref in resid_ref:
        ref[...] = two


def second_norm(x, mine, came, gain, which, keep):
    rows, width = x.shape[0] // 2, x.shape[1]
    tile = rows // 4

    def plain(start):
        return pl.BlockSpec((tile, width), lambda i: (i + 4 * start, 0))

    return call(
        second_norm_body,
        "second_norm",
        (4,),
        [plain(which), plain(which), plain(1 - which), whole(gain)],
        [plain(0)] * (1 + keep),
        [shape(rows, width), shape(rows, width, F32)][: 1 + keep],
        scalars=0,
    )(x, mine, came, gain)


def feed_forward_body(count, held, idx, *refs):
    x_refs, ct_refs = refs[:2], refs[2:4]
    gate_hbm, up_hbm, down_hbm = refs[4:7]
    refs = refs[7 + held :]
    act_ref, d_gate_ref, d_up_ref, term_a, term_b, d_a, d_b, gate_ref, up_ref, down_ref, sems = refs
    step = pl.program_id(0)
    first = step < count
    units = gate_ref.shape[1]
    mine = pl.ds(pl.multiple_of(idx[0] * units, 128), units)
    copies = [
        pltpu.make_async_copy(gate_hbm.at[:, mine], gate_ref, sems.at[0]),
        pltpu.make_async_copy(up_hbm.at[:, mine], up_ref, sems.at[1]),
        pltpu.make_async_copy(down_hbm.at[mine, :], down_ref, sems.at[2]),
    ]

    def there(copy):
        @pl.when(step == 0)
        def _():
            copy.wait()

    @pl.when(step == 0)
    def _():
        for copy in copies:
            copy.start()

    x = jnp.where(first, x_refs[0][...], x_refs[1][...])
    upstream = jnp.where(first, ct_refs[0][...], ct_refs[1][...])
    there(copies[0])
    gate = dot(x, gate_ref[...])
    there(copies[1])
    up_value = dot(x, up_ref[...])
    there(copies[2])
    d_act = dot_nt(upstream, down_ref[...])
    sigma = jax.nn.sigmoid(gate)
    silu_gate = gate * sigma
    act = (silu_gate * up_value).astype(LOW)
    d_gate = (d_act * up_value * (sigma * (1.0 + gate * (1.0 - sigma)))).astype(LOW)
    d_up = (d_act * silu_gate).astype(LOW)
    act_ref[...] = act
    d_gate_ref[...] = d_gate
    d_up_ref[...] = d_up
    d_normed = (dot_nt(d_gate, gate_ref[...]) + dot_nt(d_up, up_ref[...])).astype(LOW)
    term = dot(act, down_ref[...]).astype(LOW)

    @pl.when(first)
    def _():
        d_a[...] = d_normed
        term_a[...] = term

    @pl.when(step >= count)
    def _():
        d_b[...] = d_normed
        term_b[...] = term


def feed_forward(idx, xs, cts, weights, total, start, held):
    gate, up, down = weights
    rows, width = xs[0].shape
    units = gate.shape[1] // 2
    count = rows // TILE

    def rowed(index):
        return pl.BlockSpec((TILE, width), index)

    def lower(i, s):
        return (jnp.minimum(i, count - 1), 0)

    def upper(i, s):
        return (jnp.maximum(i - count, 0), 0)

    any_spec = pl.BlockSpec(memory_space=pl.ANY)
    unit_spec = pl.BlockSpec((TILE, units), lambda i, s: (i + start, 0))
    return call(
        functools.partial(feed_forward_body, count, len(held)),
        "feed_forward",
        (2 * count,),
        [rowed(lower), rowed(upper)] * 2 + [any_spec] * (3 + len(held)),
        [unit_spec] * 3 + [rowed(lower), rowed(upper)] * 2,
        [shape(total, units)] * 3 + [shape(rows, width)] * 4,
        [
            pltpu.VMEM((width, units), LOW),
            pltpu.VMEM((width, units), LOW),
            pltpu.VMEM((units, width), LOW),
            pltpu.SemaphoreType.DMA((3,)),
        ],
        aliases={8 + k: k for k in range(len(held))},
    )(idx, *xs, *cts, gate, up, down, *held)


def slot_masks(order):
    masks = [0]
    for link in reversed(order):
        masks = masks + [mask ^ link for mask in masks]
    return masks


def grads_body(pieces, count, chips, slots, *refs):
    x_hbm, refs = refs[:pieces], refs[pieces:]
    y_hbm, refs = refs[:count], refs[count:]
    outs, refs = refs[: 2 * count], refs[2 * count :]
    x_buf, y_buf, acc, out_buf, x_sems, y_sems, out_sems = refs
    depth = x_buf.shape[1]

    def x_copy(k):
        return pltpu.make_async_copy(x_hbm[k], x_buf.at[k], x_sems.at[k])

    def y_copy(a, k):
        rows = pl.ds(k * depth, depth)
        return pltpu.make_async_copy(y_hbm[a].at[rows], y_buf.at[a, k], y_sems.at[a, k])

    for k in range(pieces):
        x_copy(k).start()
        y_copy(0, k).start()
    for a in range(1, count):
        for k in range(pieces):
            y_copy(a, k).start()
    rows = acc.shape[0] // chips
    send_first = chips // 2
    out_copies = []
    for a in range(count):
        for k in range(pieces):
            if a == 0:
                x_copy(k).wait()
            y_copy(a, k).wait()
            term = dot_tn(x_buf[k], y_buf[a, k])
            if k == 0:
                acc[...] = term
            else:
                acc[...] += term
        for slot in range(chips):
            where = pl.ds(pl.multiple_of(slots[a * chips + slot] * rows, rows), rows)
            out_buf[a, slot] = acc[where, :].astype(LOW)
        sent = pltpu.make_async_copy(out_buf.at[a, pl.ds(send_first, chips // 2)], outs[2 * a], out_sems.at[a, 0])
        kept = pltpu.make_async_copy(out_buf.at[a, pl.ds(0, send_first)], outs[2 * a + 1], out_sems.at[a, 1])
        sent.start()
        kept.start()
        out_copies += [sent, kept]
    for copy in out_copies:
        copy.wait()


def weight_grads(slots, chips, xs, ys):
    depth, width = xs[0].shape
    units = ys[0].shape[1]
    pieces, count = len(xs), len(ys)
    any_spec = pl.BlockSpec(memory_space=pl.ANY)
    out = jax.ShapeDtypeStruct((chips // 2, width // chips, units), LOW)
    return call(
        functools.partial(grads_body, pieces, count, chips),
        "weight_grads",
        (),
        [any_spec] * (pieces + count),
        [any_spec] * (2 * count),
        [out] * (2 * count),
        [
            pltpu.VMEM((pieces, depth, width), LOW),
            pltpu.VMEM((count, pieces, depth, units), LOW),
            pltpu.VMEM((width, units), F32),
            pltpu.VMEM((count, chips, width // chips, units), LOW),
            pltpu.SemaphoreType.DMA((pieces,)),
            pltpu.SemaphoreType.DMA((count, pieces)),
            pltpu.SemaphoreType.DMA((count, 2)),
        ],
    )(slots, *xs, *ys)


def norm_back(upstream, values, scale, gain):
    scaled = values * scale
    weighted = upstream * gain
    inner = jnp.mean(weighted * scaled, axis=-1, keepdims=True)
    return scale * (weighted - scaled * inner), upstream * scaled


def resid_back_body(mine_ref, near_ref, far_ref, two_ref, cot_ref, gain_ref, d_ref, low_ref, sum_ref):
    step = pl.program_id(0)
    upstream = mine_ref[...].astype(F32) + near_ref[...].astype(F32) + far_ref[...].astype(F32)
    two = two_ref[...]
    scale = lax.rsqrt(jnp.mean(two * two, axis=-1, keepdims=True) + EPS)
    back, terms = norm_back(upstream, two, scale, gain_ref[...])
    d_resid = cot_ref[...].astype(F32) + back
    d_ref[...] = d_resid
    low_ref[...] = d_resid.astype(LOW)
    part = jnp.sum(terms.reshape(-1, 8, terms.shape[1]), axis=0)

    @pl.when(step == 0)
    def _():
        sum_ref[...] = part

    @pl.when(step > 0)
    def _():
        sum_ref[...] += part


def resid_back(mine, near, far, two, cot, gain):
    rows, width = two.shape

    def plain(kind=None):
        return pl.BlockSpec((TILE, width), lambda i: (i, 0))

    return call(
        resid_back_body,
        "resid_back",
        (rows // TILE,),
        [plain()] * 5 + [whole(gain)],
        [plain(), plain(), pl.BlockSpec((8, width), lambda i: (0, 0))],
        [shape(rows, width, F32), shape(rows, width), shape(8, width, F32)],
        scalars=0,
    )(mine, near, far, two, cot, gain)


def conv_back_body(
    block,
    count,
    chips,
    idx,
    slots,
    own_ref,
    other_ref,
    edge_ref,
    normed_ref,
    mixed_ref,
    parts_ref,
    conv_in_ref,
    conv_out_ref,
    c_edge_ref,
    in_ref,
    out_ref,
    r0,
    r1,
    r2,
    r3,
    taps_ref,
    keep_ref,
    own_normed_ref,
    other_normed_ref,
    taps_out_ref,
    send_a,
    keep_a,
    send_b,
    keep_b,
    held,
    edge_d,
    acc,
    d_proj,
    in_acc,
    out_acc,
    bufs,
    sems,
):
    step = pl.program_id(0)
    place = idx[1]
    far = (r0, r1, r2, r3)
    depth = r0.shape[1]
    half = r0.shape[2]
    cols = 2 * half

    def back_out(load):
        mine = dot_nt(load(slice(None)), out_ref[...])
        other = None
        for p in range(4):
            term = dot_nt(load(piece_columns(place, p, depth)), far[p][3])
            other = term if other is None else other + term
        return jnp.concatenate([mine, other], axis=1)

    @pl.when(step == 0)
    def _():
        edge_d[...] = back_out(lambda columns: edge_ref[:, columns]) * c_edge_ref[...]
        in_acc[...] = jnp.zeros_like(in_acc)
        out_acc[...] = jnp.zeros_like(out_acc)
        taps_out_ref[...] = jnp.zeros_like(taps_out_ref)

    held[...] = jnp.where(step < count, own_ref[...], other_ref[...])
    d_mixed = back_out(lambda columns: held[:, columns])
    d_conv = d_mixed * parts_ref[:, cols : 2 * cols].astype(F32)
    d_proj[:, cols : 2 * cols] = (d_mixed * conv_out_ref[...].astype(F32)).astype(LOW)
    groups = own_ref.shape[0] // block
    row = lax.broadcasted_iota(jnp.int32, (block, cols), 0)
    for g in range(groups):
        span = slice(g * block, (g + 1) * block)
        here = d_conv[span]
        base = step * 2 * groups + 2 * g
        after_one = edge_d[pl.ds(base, 1), :]
        after_two = edge_d[pl.ds(base + 1, 1), :]
        next_one = jnp.where(row == block - 1, after_one, pltpu.roll(here, block - 1, 0))
        next_two = jnp.where(
            row == block - 1,
            after_two,
            jnp.where(row == block - 2, after_one, pltpu.roll(here, block - 2, 0)),
        )
        next_one = keep_ref[span, 2:3] * next_one
        next_two = keep_ref[span, 3:4] * next_two
        d_in = taps_ref[2:3, :] * here + taps_ref[1:2, :] * next_one + taps_ref[0:1, :] * next_two
        conv_in = conv_in_ref[span, :].astype(F32)
        for k, term in enumerate((next_two, next_one, here)):
            taps_out_ref[k] += jnp.sum((term * conv_in).reshape(-1, 8, cols), axis=0)
        d_proj[span, :cols] = (d_in * parts_ref[span, 2 * cols :].astype(F32)).astype(LOW)
        d_proj[span, 2 * cols :] = (d_in * parts_ref[span, :cols].astype(F32)).astype(LOW)
    out_acc[...] += dot_tn(held[...], mixed_ref[...])
    in_acc[...] += dot_tn(normed_ref[...], d_proj[...])
    total = None
    for j in range(3):
        term = dot_nt(d_proj[:, j * cols : j * cols + half], in_ref[j])
        total = term if total is None else total + term
    acc[...] = total
    for p in range(4):
        where = piece_columns(place, p, depth)
        total = None
        for j in range(3):
            term = dot_nt(d_proj[:, j * cols + half : (j + 1) * cols], far[p][j])
            total = term if total is None else total + term
        acc[:, where] += total

    @pl.when(step < count)
    def _():
        own_normed_ref[...] = acc[...].astype(LOW)

    @pl.when(step >= count)
    def _():
        other_normed_ref[...] = acc[...].astype(LOW)

    @pl.when(step == 2 * count - 1)
    def _():
        rows = in_acc.shape[0] // chips
        copies = []
        for a, (halves, keeps, sends) in enumerate(
            (
                (((out_acc, 0), (in_acc, 0)), keep_a, send_a),
                (((in_acc, cols), (in_acc, 2 * cols)), keep_b, send_b),
            )
        ):
            for slot in range(2 * chips):
                number = a * 2 * chips + slot
                where = pl.ds(pl.multiple_of(slots[number] * rows, rows), rows)
                other = slot_pair(a, slot, chips)
                for at, (source, start) in enumerate(halves):
                    low = start + other * half
                    bufs[a, slot, :, at * half : (at + 1) * half] = source[
                        where, low : low + half
                    ].astype(LOW)
            sent = pltpu.make_async_copy(bufs.at[a, pl.ds(chips, chips)], sends, sems.at[a, 0])
            kept = pltpu.make_async_copy(bufs.at[a, pl.ds(0, chips)], keeps, sems.at[a, 1])
            sent.start()
            kept.start()
            copies += [sent, kept]
        for copy in copies:
            copy.wait()


def slot_pair(group, slot, chips):
    return slot // chips if group == 0 else (slot // (chips // 2)) % 2


def mix_orders(links):
    return ["pair"] + links, [links[0], "pair"] + links[1:]


def conv_back(idx, slots, chips, own, other, edges, kept, in_weight, out_weight, far, taps, keeps, block):
    normed_mix, parts, conv_in, conv_out, mixed, c_edge = kept
    rows, width = own.shape
    half = far[0].shape[2]
    cols = 2 * half
    tile = TILE
    count = rows // tile

    def rowed(columns):
        return pl.BlockSpec((tile, columns), lambda i, s, t: (i, 0))

    def fixed(array):
        zeros = (0,) * array.ndim
        return pl.BlockSpec(array.shape, lambda i, s, t: zeros)

    lower = pl.BlockSpec((tile, width), lambda i, s, t: (jnp.minimum(i, count - 1), 0))
    upper = pl.BlockSpec((tile, width), lambda i, s, t: (jnp.maximum(i - count, 0), 0))
    any_spec = pl.BlockSpec(memory_space=pl.ANY)
    grad = jax.ShapeDtypeStruct((chips, width // chips, cols), LOW)
    return call(
        functools.partial(conv_back_body, block, count, chips),
        "conv_back",
        (2 * count,),
        [
            lower,
            upper,
            fixed(edges),
            rowed(width),
            rowed(cols),
            rowed(3 * cols),
            rowed(cols),
            rowed(cols),
            fixed(c_edge),
            pl.BlockSpec((3, width, half), lambda i, s, t: (0, 0, s[0])),
            pl.BlockSpec((half, width), lambda i, s, t: (s[0], 0)),
            *[fixed(piece) for piece in far],
            fixed(taps),
            rowed(keeps.shape[1]),
        ],
        [lower, upper, pl.BlockSpec((3, 8, cols), lambda i, s, t: (0, 0, 0))] + [any_spec] * 4,
        [
            shape(rows, width),
            shape(rows, width),
            jax.ShapeDtypeStruct((3, 8, cols), F32),
        ]
        + [grad] * 4,
        [
            pltpu.VMEM((tile, width), LOW),
            pltpu.VMEM((edges.shape[0], cols), F32),
            pltpu.VMEM((tile, width), F32),
            pltpu.VMEM((tile, 3 * cols), LOW),
            pltpu.VMEM((width, 3 * cols), F32),
            pltpu.VMEM((width, cols), F32),
            pltpu.VMEM((2, 2 * chips, width // chips, cols), LOW),
            pltpu.SemaphoreType.DMA((2, 2)),
        ],
        scalars=2,
    )(
        idx,
        slots,
        own,
        other,
        edges,
        normed_mix,
        mixed,
        parts,
        conv_in,
        conv_out,
        c_edge,
        in_weight,
        out_weight,
        *far,
        taps,
        keeps,
    )


def hidden_back_body(mine_ref, came_ref, x_ref, d_ref, gain_ref, out_ref, sum_ref):
    step = pl.program_id(0)
    upstream = mine_ref[...].astype(F32) + came_ref[...].astype(F32)
    resid = x_ref[...].astype(F32)
    scale = lax.rsqrt(jnp.mean(resid * resid, axis=-1, keepdims=True) + EPS)
    back, terms = norm_back(upstream, resid, scale, gain_ref[...])
    out_ref[...] = d_ref[...] + back
    part = jnp.sum(terms.reshape(-1, 8, terms.shape[1]), axis=0)

    @pl.when(step == 0)
    def _():
        sum_ref[...] = part

    @pl.when(step > 0)
    def _():
        sum_ref[...] += part


def hidden_back(mine, came, x, d_resid, gain):
    rows, width = x.shape
    plain = pl.BlockSpec((TILE, width), lambda i: (i, 0))
    return call(
        hidden_back_body,
        "hidden_back",
        (rows // TILE,),
        [plain] * 4 + [whole(gain)],
        [plain, pl.BlockSpec((8, width), lambda i: (0, 0))],
        [shape(rows, width, F32), shape(8, width, F32)],
        scalars=0,
    )(mine, came, x, d_resid, gain)


class Halving:
    def __init__(self, keep, order):
        self.terms = [keep]
        self.half = keep.shape[0]
        self.links = list(order)

    def start(self, send):
        self.terms.append(swap(send, self.links.pop(0)))

    def step(self, *after):
        self.half //= 2
        half = self.half
        terms = self.terms
        if after:
            terms = [tie(terms[0], *after)] + terms[1:]
        going = sum(term[half : 2 * half].astype(F32) for term in terms).astype(LOW)
        self.terms.append(swap(going, self.links.pop(0)))

    def done(self):
        return sum(term[0].astype(F32) for term in self.terms)


def local(
    hidden,
    segments,
    cotangent,
    in_weight,
    out_weight,
    gate_weight,
    up_weight,
    down_weight,
    conv_weight,
    norm_mix,
    norm_ffn,
):
    groups, block, width = hidden.shape
    rows = groups * block
    size = lax.axis_size("seq")
    seq_index = lax.axis_index("seq")
    core = seq_index % 2
    chip = seq_index // 2
    pair = lax.axis_index("wshard")
    first_core = core == 0
    chips = size // 2
    links = [1 << bit for bit in range(chips.bit_length() - 1)]
    turned = [links[1], links[0]] + links[2:]
    half = out_weight.shape[0] // 2
    cols = 2 * half
    place = chip & 3
    idx = jnp.stack([core, place]).astype(jnp.int32)

    def slots_of(*orders):
        masks = [mask for order in orders for mask in slot_masks(order)]
        return (chip ^ jnp.array(masks, jnp.int32)).astype(jnp.int32)

    weights = (gate_weight, up_weight, down_weight)

    def ordered(flag, mine, other, axis):
        return jnp.where(
            flag,
            jnp.concatenate([mine, other], axis=axis),
            jnp.concatenate([other, mine], axis=axis),
        )

    small = jnp.concatenate([conv_weight, norm_mix[None], norm_ffn[None]], axis=0)
    in_planes = jnp.transpose(in_weight, (1, 0, 2))
    depth = width // 4

    def piece(number):
        from_in = lax.dynamic_slice(in_planes, (0, number * depth, core * half), (3, depth, half))
        from_out = lax.dynamic_slice(out_weight, (core * half, number * depth), (half, depth))
        return jnp.concatenate([from_in, from_out[None]], axis=0)

    sent_zero = piece(place)
    sent_three = piece(place ^ 3)
    piece_zero = swap_pair(sent_zero)
    piece_three = swap_pair(sent_three)
    small_other = swap_pair(tie(small, sent_zero))
    piece_one = swap(piece_zero, 1)
    piece_two = swap(piece_zero, 2)
    far_weights = (piece_zero, piece_one, piece_two, piece_three)

    hidden, segments = lax.optimization_barrier((hidden, segments, sent_zero, sent_three))[:2]
    own = hidden.reshape(rows, width)
    other = swap_core(own)
    chip_hidden = jnp.concatenate([own, other], axis=0)
    cot = cotangent.reshape(rows, width)
    cot_far = swap_pair(tie(cot, piece_zero))

    seg_low = segments.astype(LOW)
    seg_other = swap_core(seg_low)

    def with_seg(values, segs):
        return jnp.concatenate(
            [values, jnp.broadcast_to(segs[:, :, None], (groups, segs.shape[1], 128))], axis=2
        )

    def ends(values, segs):
        both = values.reshape(groups, block, width)
        return (
            with_seg(both[:, :2], segs[:, :2]),
            with_seg(both[:, block - 2 :], segs[:, block - 2 :]),
        )

    head, last = ends(own, seg_low)
    other_head, other_last = ends(other, seg_other)
    even = range(2, size, 2)
    forth = [(i - 2, i) for i in range(2, size)]
    back = [(i, i - 2) for i in range(2, size)]
    from_before = over_seq(jnp.where(first_core, other_last, last), forth)
    from_after = over_seq(jnp.where(first_core, head, other_head), back)

    def after_blocks(outside, own_head, near_head):
        return jnp.where(
            first_core, jnp.stack([near_head, outside]), jnp.stack([outside, own_head])
        )

    before = jnp.where(
        first_core, jnp.stack([from_before, last]), jnp.stack([other_last, from_before])
    )
    after = after_blocks(from_after, head, other_head)
    edges = jnp.concatenate([before, after], axis=0)
    edge_rows = edges[..., :width].reshape(8 * groups, width)
    edge_segs = edges[..., width]
    segs = jnp.stack([seg_low, seg_other])
    segs_ext = jnp.concatenate([edge_segs[:2], segs, edge_segs[2:]], axis=2)
    keeps = jnp.stack(
        [(segs_ext[:, :, at : at + block] == segs).astype(F32) for at in (1, 0, 3, 4)], axis=-1
    ).reshape(2 * rows, 4)

    gains = ordered(pair == 0, small[3:], small_other[3:], 1).astype(F32)
    gain_mix, gain_ffn = gains[:1], gains[1:]
    taps = jnp.concatenate(
        [lax.dynamic_slice_in_dim(part[:3], core * half, half, 1) for part in (small, small_other)],
        axis=1,
    ).astype(F32)

    normed_mix, parts, conv_in, conv_out, mixed, mix_part, c_edge = conv_forward(
        idx, chip_hidden, edge_rows, in_planes, out_weight, far_weights, gain_mix, taps, keeps, block
    )
    mix_came = swap_core(mix_part)
    own_x, resid_two = second_norm(chip_hidden, mix_part, mix_came, gain_ffn, 0, True)
    far_x = swap_pair(own_x)
    other_x = second_norm(tie(chip_hidden, own_x), mix_part, mix_came, gain_ffn, 1, False)[0]

    cot_other = swap_core(cot)
    cot_diag = swap_core(tie(cot_far, mix_came))
    total = 4 * rows
    act, d_gate, d_up, term_own, term_other, d_own, d_other = feed_forward(
        idx, [own_x, other_x], [cot, cot_other], weights, total, 0, ()
    )
    diag_x = swap_core(tie(far_x, d_own))
    near_d = swap_core(d_other)
    near_term = swap_core(term_other)
    act, d_gate, d_up, term_far, term_diag, d_far, d_diag = feed_forward(
        idx,
        [far_x, diag_x],
        [cot_far, cot_diag],
        weights,
        total,
        2 * rows // TILE,
        (act, d_gate, d_up),
    )
    d_diag_came = swap_core(d_diag)
    down_send, down_keep = weight_grads(
        slots_of(links), chips, [cot, cot_other, cot_far, cot_diag], [act]
    )
    sum_down = Halving(down_keep, links)
    sum_down.start(down_send)
    home = swap_pair(
        (d_far.astype(F32) + tie(d_diag_came, down_send).astype(F32)).astype(LOW)
    )
    term_home = swap_pair(
        (term_far.astype(F32) + swap_core(tie(term_diag, down_send)).astype(F32)).astype(LOW)
    )
    gate_send, gate_keep, up_send, up_keep = weight_grads(
        slots_of(turned, links), chips, [own_x, other_x, far_x, diag_x], [d_gate, tie(d_up, down_send)]
    )
    sum_gate = Halving(gate_keep, turned)
    sum_gate.start(gate_send)
    sum_up = Halving(up_keep, links)
    sum_up.start(up_send)

    d_resid, d_low, gain_ffn_terms = resid_back(d_own, near_d, home, resid_two, cot, gain_ffn)
    d_near = swap_core(d_low)
    d_head = d_low.reshape(groups, block, width)[:, :2]
    d_after = jnp.where(
        first_core,
        over_seq(d_head, [(i, i - 2) for i in even]),
        over_seq(d_head, [(i, i - 1) for i in even]),
    )
    d_edges = after_blocks(
        d_after, d_head, d_near.reshape(groups, block, width)[:, :2]
    ).reshape(4 * groups, width)
    sum_down.step(d_low)
    orders = mix_orders(links)
    slots_mix = slots_of(
        *[[0 if link == "pair" else link for link in order] for order in orders]
    )
    d_normed_own, d_normed_other, tap_terms, send_a, keep_a, send_b, keep_b = conv_back(
        idx,
        slots_mix,
        chips,
        d_low,
        d_near,
        d_edges,
        (normed_mix, parts, conv_in, conv_out, mixed, c_edge),
        in_planes,
        out_weight,
        far_weights,
        taps,
        keeps,
        block,
    )
    sum_a = Halving(keep_a, orders[0])
    sum_b = Halving(keep_b, orders[1])
    sum_a.start(send_a)
    sum_b.start(send_b)
    d_normed_came = swap_core(d_normed_other)
    sum_gate.step(send_a)
    sum_up.step(send_a)
    sum_down.step(send_a)
    grad_hidden, gain_mix_terms = hidden_back(
        d_normed_own, d_normed_came, own, d_resid, gain_mix
    )

    taps_sum = jnp.sum(tap_terms, axis=1)
    half_width = norm_mix.shape[0]
    spread = jnp.zeros((3, width), F32)
    spread = lax.dynamic_update_slice_in_dim(
        spread, taps_sum[:, :half], pair * half_width + core * half, 1
    )
    spread = lax.dynamic_update_slice_in_dim(
        spread, taps_sum[:, half:], (1 - pair) * half_width + core * half, 1
    )
    sums = jnp.concatenate(
        [
            spread,
            jnp.sum(gain_mix_terms, axis=0, keepdims=True),
            jnp.sum(gain_ffn_terms, axis=0, keepdims=True),
        ],
        axis=0,
    )
    sums = sums + swap_core(sums)
    for link in ["pair"] + links:
        sums = sums + swap(sums, link)
    sums = lax.dynamic_slice_in_dim(sums, pair * half_width, half_width, 1)
    for reduction in (sum_down, sum_gate, sum_up):
        while reduction.links:
            reduction.step(grad_hidden)
    while sum_a.links:
        sum_a.step()
        sum_b.step()

    block_out = (
        resid_two
        + (term_own.astype(F32) + near_term.astype(F32) + tie(term_home, send_a).astype(F32))
    ).astype(LOW)

    part_rows = width // size

    def finish(reductions):
        total = jnp.concatenate([reduction.done() for reduction in reductions], axis=1)
        total = total.reshape(2, part_rows, -1)
        came = swap_core(
            jnp.where(first_core, total[1], total[0]).astype(LOW)
        ).astype(F32)
        mine = jnp.where(first_core, total[0], total[1])
        each = mine.shape[1] // (3 if len(reductions) == 3 else 4)
        return [
            ordered(first_core, mine[:, at : at + each], came[:, at : at + each], 1)
            for at in range(0, mine.shape[1], each)
        ]

    out_down, out_gate, out_up = finish([sum_down, sum_gate, sum_up])
    out_out, out_b, out_c, out_x = finish([sum_a, sum_b])
    return (
        block_out.reshape(groups, block, width),
        grad_hidden.reshape(groups, block, width),
        jnp.stack([out_b, out_c, out_x], axis=1),
        out_out.T,
        out_gate,
        out_up,
        out_down.T,
        sums[:3],
        sums[3],
        sums[4],
    )


def solution(mesh):
    return jax.shard_map(
        local,
        mesh=mesh,
        in_specs=(
            P("wshard", "seq", None),
            P("wshard", "seq"),
            P("wshard", "seq", None),
            P(None, None, "wshard"),
            P("wshard", None),
            P(None, "wshard"),
            P(None, "wshard"),
            P("wshard", None),
            P(None, "wshard"),
            P("wshard"),
            P("wshard"),
        ),
        out_specs=(
            P("wshard", "seq", None),
            P("wshard", "seq", None),
            P("seq", None, "wshard"),
            P("wshard", "seq"),
            P("seq", "wshard"),
            P("seq", "wshard"),
            P("wshard", "seq"),
            P(None, "wshard"),
            P("wshard"),
            P("wshard"),
        ),
        check_vma=False,
    )
```

```python
import functools

import jax
import jax.numpy as jnp
from jax import lax
from jax.experimental import pallas as pl
from jax.experimental.pallas import tpu as pltpu
from jax.sharding import PartitionSpec as P

EPS = 1e-05
LOW = jnp.bfloat16
F32 = jnp.float32
TILE = 256
NT = (((1,), (1,)), ((), ()))
TN = (((0,), (0,)), ((), ()))


def over_seq(block, route):
    return lax.ppermute(block, "seq", route)


def swap_seq(block, mask):
    return over_seq(block, [(i, i ^ mask) for i in range(lax.axis_size("seq"))])


def swap_core(block):
    return swap_seq(block, 1)


def swap_pair(block):
    return lax.ppermute(block, "wshard", [(0, 1), (1, 0)])


def swap(block, link):
    return swap_pair(block) if link == "pair" else swap_seq(block, 2 * link)


def tie(value, *after):
    return lax.optimization_barrier((value,) + after)[0]


def dot(left, right):
    return jnp.dot(left, right, preferred_element_type=F32)


def dot_nt(left, right):
    return lax.dot_general(left, right, NT, preferred_element_type=F32)


def dot_tn(left, right):
    return lax.dot_general(left, right, TN, preferred_element_type=F32)


def call(
    body, name, grid, in_specs, out_specs, out_shape, scratch=(), scalars=1, aliases=None, mib=36
):
    return pl.pallas_call(
        body,
        grid_spec=pltpu.PrefetchScalarGridSpec(
            num_scalar_prefetch=scalars,
            grid=grid,
            in_specs=in_specs,
            out_specs=out_specs,
            scratch_shapes=list(scratch),
        ),
        out_shape=out_shape,
        input_output_aliases=aliases or {},
        compiler_params=pltpu.CompilerParams(vmem_limit_bytes=mib * 2**20),
        cost_estimate=pl.CostEstimate(flops=1000, bytes_accessed=1000, transcendentals=0),
        name=name,
    )


def shape(rows, cols, kind=LOW):
    return jax.ShapeDtypeStruct((rows, cols), kind)


def whole(array):
    zeros = (0,) * array.ndim
    return pl.BlockSpec(array.shape, lambda *_: zeros)


def normed(values, gain):
    wide = values.astype(F32)
    scale = lax.rsqrt(jnp.mean(wide * wide, axis=-1, keepdims=True) + EPS)
    return wide * scale * gain, scale


def piece_columns(place, j, depth):
    return pl.ds(pl.multiple_of((place ^ j) * depth, depth), depth)


def conv_forward_body(
    block,
    idx,
    x_ref,
    edge_ref,
    in_ref,
    out_ref,
    r0,
    r1,
    r2,
    r3,
    gain_ref,
    taps_ref,
    keep_ref,
    normed_ref,
    parts_ref,
    conv_in_ref,
    conv_out_ref,
    mixed_ref,
    own_mix_ref,
    other_mix_ref,
    c_edge_ref,
    nx,
    edge_in,
    acc,
):
    step = pl.program_id(0)
    place = idx[1]
    far = (r0, r1, r2, r3)
    depth = r0.shape[1]
    half = r0.shape[2]
    cols = 2 * half
    gain = gain_ref[...]

    def project(load, j):
        mine = dot(load(slice(None)), in_ref[j])
        other = None
        for p in range(4):
            term = dot(load(piece_columns(place, p, depth)), far[p][j])
            other = term if other is None else other + term
        return jnp.concatenate([mine, other], axis=1)

    @pl.when(step == 0)
    def _():
        count = edge_ref.shape[0]
        nx[:count] = normed(edge_ref[...], gain)[0].astype(LOW)

        def load(columns):
            return nx[:count, columns]

        before = count // 2
        edge_b, edge_c, edge_x = (project(load, j) for j in range(3))
        edge_in[...] = (edge_b[:before] * edge_x[:before]).astype(LOW).astype(F32)
        c_edge_ref[...] = edge_c[before:]

    nx[...] = normed(x_ref[...], gain)[0].astype(LOW)
    normed_ref[...] = nx[...]

    def load(columns):
        return nx[:, columns]

    b_part, c_part, x_part = (project(load, j) for j in range(3))
    parts_ref[:, :cols] = b_part.astype(LOW)
    parts_ref[:, cols : 2 * cols] = c_part.astype(LOW)
    parts_ref[:, 2 * cols :] = x_part.astype(LOW)
    low_in = (b_part * x_part).astype(LOW)
    conv_in_ref[...] = low_in
    conv_in = low_in.astype(F32)
    groups = x_ref.shape[0] // block
    row = lax.broadcasted_iota(jnp.int32, (block, cols), 0)
    for g in range(groups):
        span = slice(g * block, (g + 1) * block)
        here = conv_in[span]
        base = step * 2 * groups + 2 * g
        two_before = edge_in[pl.ds(base, 1), :]
        one_before = edge_in[pl.ds(base + 1, 1), :]
        lag_one = jnp.where(row == 0, one_before, pltpu.roll(here, 1, 0))
        lag_two = jnp.where(
            row == 0, two_before, jnp.where(row == 1, one_before, pltpu.roll(here, 2, 0))
        )
        conv_out = (
            taps_ref[2:3, :] * here
            + taps_ref[1:2, :] * (keep_ref[span, 0:1] * lag_one)
            + taps_ref[0:1, :] * (keep_ref[span, 1:2] * lag_two)
        )
        conv_out_ref[span, :] = conv_out.astype(LOW)
        mixed_ref[span, :] = (c_part[span] * conv_out).astype(LOW)
    mixed = mixed_ref[...]
    acc[...] = dot(mixed[:, :half], out_ref[...])
    for p in range(4):
        where = piece_columns(place, p, depth)
        acc[:, where] += dot(mixed[:, half:], far[p][3])
    mix = acc[...].astype(LOW)
    count = pl.num_programs(0) // 2

    @pl.when(step < count)
    def _():
        own_mix_ref[...] = mix

    @pl.when(step >= count)
    def _():
        other_mix_ref[...] = mix


def conv_forward(idx, x, edges, in_weight, out_weight, far, gain, taps, keeps, block):
    total, width = x.shape
    rows = TILE
    half = far[0].shape[2]
    cols = 2 * half

    def rowed(columns):
        return pl.BlockSpec((rows, columns), lambda i, s: (i, 0))

    before = edges.shape[0] // 2
    count = total // rows // 2
    return call(
        functools.partial(conv_forward_body, block),
        "conv_forward",
        (total // rows,),
        [
            rowed(width),
            whole(edges),
            pl.BlockSpec((3, width, half), lambda i, s: (0, 0, s[0])),
            pl.BlockSpec((half, width), lambda i, s: (s[0], 0)),
            *[whole(piece) for piece in far],
            whole(gain),
            whole(taps),
            rowed(keeps.shape[1]),
        ],
        [
            rowed(width),
            rowed(3 * cols),
            rowed(cols),
            rowed(cols),
            rowed(cols),
            pl.BlockSpec((rows, width), lambda i, s: (jnp.minimum(i, count - 1), 0)),
            pl.BlockSpec((rows, width), lambda i, s: (jnp.maximum(i - count, 0), 0)),
            pl.BlockSpec((before, cols), lambda i, s: (0, 0)),
        ],
        [
            pltpu.HBM((total, width), LOW),
            pltpu.HBM((total, 3 * cols), LOW),
            pltpu.HBM((total, cols), LOW),
            pltpu.HBM((total, cols), LOW),
            pltpu.HBM((total, cols), LOW),
            shape(total // 2, width),
            shape(total // 2, width),
            shape(before, cols, F32),
        ],
        [
            pltpu.VMEM((rows, width), LOW),
            pltpu.VMEM((before, cols), F32),
            pltpu.VMEM((rows, width), F32),
        ],
    )(idx, x, edges, in_weight, out_weight, *far, gain, taps, keeps)


def second_norm_body(x_ref, mine_ref, came_ref, gain_ref, low_ref, *resid_ref):
    two = x_ref[...].astype(F32) + (mine_ref[...].astype(F32) + came_ref[...].astype(F32))
    low_ref[...] = normed(two, gain_ref[...])[0].astype(LOW)
    for ref in resid_ref:
        ref[...] = two


def second_norm(x, mine, came, gain, which, keep):
    rows, width = mine.shape
    tile = rows // 4

    def plain(start):
        return pl.BlockSpec((tile, width), lambda i: (i + 4 * start, 0))

    return call(
        second_norm_body,
        "second_norm",
        (4,),
        [plain(which), plain(0), plain(0), whole(gain)],
        [plain(0)] * (1 + keep),
        [shape(rows, width), pltpu.HBM((rows, width), F32)][: 1 + keep],
        scalars=0,
        mib=12,
    )(x, mine, came, gain)


def feed_forward_body(count, held, idx, *refs):
    x_refs, ct_refs = refs[:2], refs[2:4]
    gate_ref, up_ref, down_ref = refs[4:7]
    refs = refs[7 + held :]
    act_ref, d_gate_ref, d_up_ref, term_a, term_b, d_a, d_b = refs
    step = pl.program_id(0)
    first = step < count
    x = jnp.where(first, x_refs[0][...], x_refs[1][...])
    upstream = jnp.where(first, ct_refs[0][...], ct_refs[1][...])
    gate = dot(x, gate_ref[...])
    up_value = dot(x, up_ref[...])
    d_act = dot_nt(upstream, down_ref[...])
    sigma = jax.nn.sigmoid(gate)
    silu_gate = gate * sigma
    act = (silu_gate * up_value).astype(LOW)
    d_gate = (d_act * up_value * (sigma * (1.0 + gate * (1.0 - sigma)))).astype(LOW)
    d_up = (d_act * silu_gate).astype(LOW)
    act_ref[...] = act
    d_gate_ref[...] = d_gate
    d_up_ref[...] = d_up
    d_normed = (dot_nt(d_gate, gate_ref[...]) + dot_nt(d_up, up_ref[...])).astype(LOW)
    term = dot(act, down_ref[...]).astype(LOW)

    @pl.when(first)
    def _():
        d_a[...] = d_normed
        term_a[...] = term

    @pl.when(step >= count)
    def _():
        d_b[...] = d_normed
        term_b[...] = term


def feed_forward(idx, xs, cts, weights, total, start, held):
    gate, up, down = weights
    rows, width = xs[0].shape
    units = gate.shape[1] // 2
    count = rows // TILE

    def rowed(index):
        return pl.BlockSpec((TILE, width), index)

    def lower(i, s):
        return (jnp.minimum(i, count - 1), 0)

    def upper(i, s):
        return (jnp.maximum(i - count, 0), 0)

    any_spec = pl.BlockSpec(memory_space=pl.ANY)
    unit_spec = pl.BlockSpec((TILE, units), lambda i, s: (i + start, 0))
    columns = pl.BlockSpec((width, units), lambda i, s: (0, s[0]))
    return call(
        functools.partial(feed_forward_body, count, len(held)),
        "feed_forward",
        (2 * count,),
        [rowed(lower), rowed(upper)] * 2
        + [columns, columns, pl.BlockSpec((units, width), lambda i, s: (s[0], 0))]
        + [any_spec] * len(held),
        [unit_spec] * 3 + [rowed(lower), rowed(upper)] * 2,
        [shape(total, units)] * 3 + [shape(rows, width)] * 4,
        aliases={8 + k: k for k in range(len(held))},
        mib=30,
    )(idx, *xs, *cts, gate, up, down, *held)


def slot_masks(order):
    masks = [0]
    for link in reversed(order):
        masks = masks + [mask ^ link for mask in masks]
    return masks


def grads_body(pieces, count, chips, slots, *refs):
    x_hbm, refs = refs[:pieces], refs[pieces:]
    y_hbm, refs = refs[:count], refs[count:]
    outs, refs = refs[: 2 * count], refs[2 * count :]
    x_buf, y_buf, acc, out_buf, x_sems, y_sems, out_sems = refs
    depth = x_buf.shape[1]

    def x_copy(k):
        return pltpu.make_async_copy(x_hbm[k], x_buf.at[k], x_sems.at[k])

    def y_copy(a, k):
        rows = pl.ds(k * depth, depth)
        return pltpu.make_async_copy(y_hbm[a].at[rows], y_buf.at[a, k], y_sems.at[a, k])

    for k in range(pieces):
        x_copy(k).start()
        y_copy(0, k).start()
    for a in range(1, count):
        for k in range(pieces):
            y_copy(a, k).start()
    rows = acc.shape[0] // chips
    send_first = chips // 2
    out_copies = []
    for a in range(count):
        for k in range(pieces):
            if a == 0:
                x_copy(k).wait()
            y_copy(a, k).wait()
        for k in range(pieces):
            term = dot_tn(x_buf[k], y_buf[a, k])
            if k == 0:
                acc[...] = term
            else:
                acc[...] += term
        for slot in range(chips):
            where = pl.ds(pl.multiple_of(slots[a * chips + slot] * rows, rows), rows)
            out_buf[a, slot] = acc[where, :].astype(LOW)
        sent = pltpu.make_async_copy(out_buf.at[a, pl.ds(send_first, chips // 2)], outs[2 * a], out_sems.at[a, 0])
        kept = pltpu.make_async_copy(out_buf.at[a, pl.ds(0, send_first)], outs[2 * a + 1], out_sems.at[a, 1])
        sent.start()
        kept.start()
        out_copies += [sent, kept]
    for copy in out_copies:
        copy.wait()


def weight_grads(slots, chips, xs, ys):
    depth, width = xs[0].shape
    units = ys[0].shape[1]
    pieces, count = len(xs), len(ys)
    any_spec = pl.BlockSpec(memory_space=pl.ANY)
    out = jax.ShapeDtypeStruct((chips // 2, width // chips, units), LOW)
    return call(
        functools.partial(grads_body, pieces, count, chips),
        "weight_grads",
        (),
        [any_spec] * (pieces + count),
        [any_spec] * (2 * count),
        [out] * (2 * count),
        [
            pltpu.VMEM((pieces, depth, width), LOW),
            pltpu.VMEM((count, pieces, depth, units), LOW),
            pltpu.VMEM((width, units), F32),
            pltpu.VMEM((count, chips, width // chips, units), LOW),
            pltpu.SemaphoreType.DMA((pieces,)),
            pltpu.SemaphoreType.DMA((count, pieces)),
            pltpu.SemaphoreType.DMA((count, 2)),
        ],
        mib=26,
    )(slots, *xs, *ys)


def norm_back(upstream, values, scale, gain):
    scaled = values * scale
    weighted = upstream * gain
    inner = jnp.mean(weighted * scaled, axis=-1, keepdims=True)
    return scale * (weighted - scaled * inner), upstream * scaled


def resid_back_body(mine_ref, near_ref, far_ref, two_ref, cot_ref, gain_ref, d_ref, low_ref, sum_ref):
    step = pl.program_id(0)
    upstream = mine_ref[...].astype(F32) + near_ref[...].astype(F32) + far_ref[...].astype(F32)
    two = two_ref[...]
    scale = lax.rsqrt(jnp.mean(two * two, axis=-1, keepdims=True) + EPS)
    back, terms = norm_back(upstream, two, scale, gain_ref[...])
    d_resid = cot_ref[...].astype(F32) + back
    d_ref[...] = d_resid
    low_ref[...] = d_resid.astype(LOW)
    part = jnp.sum(terms.reshape(-1, 8, terms.shape[1]), axis=0)

    @pl.when(step == 0)
    def _():
        sum_ref[...] = part

    @pl.when(step > 0)
    def _():
        sum_ref[...] += part


def resid_back(mine, near, far, two, cot, gain):
    rows, width = two.shape

    def plain(kind=None):
        return pl.BlockSpec((TILE, width), lambda i: (i, 0))

    return call(
        resid_back_body,
        "resid_back",
        (rows // TILE,),
        [plain()] * 5 + [whole(gain)],
        [plain(), plain(), pl.BlockSpec((8, width), lambda i: (0, 0))],
        [shape(rows, width, F32), shape(rows, width), shape(8, width, F32)],
        scalars=0,
        mib=16,
    )(mine, near, far, two, cot, gain)


def conv_back_body(
    block,
    count,
    chips,
    idx,
    slots,
    own_ref,
    other_ref,
    edge_ref,
    x_ref,
    gain_terms_ref,
    normed_ref,
    mixed_ref,
    parts_ref,
    conv_in_ref,
    conv_out_ref,
    c_edge_ref,
    in_ref,
    out_ref,
    r0,
    r1,
    r2,
    r3,
    taps_ref,
    keep_ref,
    own_normed_ref,
    other_normed_ref,
    sums_ref,
    send_a,
    keep_a,
    send_b,
    keep_b,
    held,
    edge_d,
    acc,
    d_proj,
    in_acc,
    out_acc,
    taps_acc,
    gain_acc,
    bufs,
    sems,
):
    step = pl.program_id(0)
    place = idx[1]
    far = (r0, r1, r2, r3)
    depth = r0.shape[1]
    half = r0.shape[2]
    cols = 2 * half

    def back_out(load):
        mine = dot_nt(load(slice(None)), out_ref[...])
        other = None
        for p in range(4):
            term = dot_nt(load(piece_columns(place, p, depth)), far[p][3])
            other = term if other is None else other + term
        return jnp.concatenate([mine, other], axis=1)

    @pl.when(step == 0)
    def _():
        edge_d[...] = back_out(lambda columns: edge_ref[:, columns]) * c_edge_ref[...]
        in_acc[...] = jnp.zeros_like(in_acc)
        out_acc[...] = jnp.zeros_like(out_acc)
        taps_acc[...] = jnp.zeros_like(taps_acc)
        gain_acc[...] = jnp.zeros_like(gain_acc)

    held[...] = jnp.where(step < count, own_ref[...], other_ref[...])
    d_mixed = back_out(lambda columns: held[:, columns])
    d_conv = d_mixed * parts_ref[:, cols : 2 * cols].astype(F32)
    d_proj[:, cols : 2 * cols] = (d_mixed * conv_out_ref[...].astype(F32)).astype(LOW)
    groups = own_ref.shape[0] // block
    row = lax.broadcasted_iota(jnp.int32, (block, cols), 0)
    for g in range(groups):
        span = slice(g * block, (g + 1) * block)
        here = d_conv[span]
        base = step * 2 * groups + 2 * g
        after_one = edge_d[pl.ds(base, 1), :]
        after_two = edge_d[pl.ds(base + 1, 1), :]
        next_one = jnp.where(row == block - 1, after_one, pltpu.roll(here, block - 1, 0))
        next_two = jnp.where(
            row == block - 1,
            after_two,
            jnp.where(row == block - 2, after_one, pltpu.roll(here, block - 2, 0)),
        )
        next_one = keep_ref[span, 2:3] * next_one
        next_two = keep_ref[span, 3:4] * next_two
        d_in = taps_ref[2:3, :] * here + taps_ref[1:2, :] * next_one + taps_ref[0:1, :] * next_two
        conv_in = conv_in_ref[span, :].astype(F32)
        for k, term in enumerate((next_two, next_one, here)):
            taps_acc[k] += jnp.sum((term * conv_in).reshape(-1, 8, cols), axis=0)
        d_proj[span, :cols] = (d_in * parts_ref[span, 2 * cols :].astype(F32)).astype(LOW)
        d_proj[span, 2 * cols :] = (d_in * parts_ref[span, :cols].astype(F32)).astype(LOW)
    out_acc[...] += dot_tn(held[...], mixed_ref[...])
    in_acc[...] += dot_tn(normed_ref[...], d_proj[...])
    total = None
    for j in range(3):
        term = dot_nt(d_proj[:, j * cols : j * cols + half], in_ref[j])
        total = term if total is None else total + term
    acc[...] = total
    for p in range(4):
        where = piece_columns(place, p, depth)
        total = None
        for j in range(3):
            term = dot_nt(d_proj[:, j * cols + half : (j + 1) * cols], far[p][j])
            total = term if total is None else total + term
        acc[:, where] += total
    wide = x_ref[...].astype(F32)
    scale = lax.rsqrt(jnp.mean(wide * wide, axis=-1, keepdims=True) + EPS)
    terms = acc[...] * (wide * scale)
    gain_acc[...] += jnp.sum(terms.reshape(-1, 8, terms.shape[1]), axis=0)

    @pl.when(step < count)
    def _():
        own_normed_ref[...] = acc[...].astype(LOW)

    @pl.when(step >= count)
    def _():
        other_normed_ref[...] = acc[...].astype(LOW)

    @pl.when(step == 2 * count - 1)
    def _():
        sums_ref[...] = jnp.zeros_like(sums_ref)
        for k in range(3):
            line = jnp.sum(taps_acc[k], axis=0, keepdims=True)
            for part in range(2):
                side = idx[2] if part == 0 else 1 - idx[2]
                at = pl.multiple_of((2 * side + idx[0]) * half, 128)
                sums_ref[k : k + 1, pl.ds(at, half)] = line[:, part * half : (part + 1) * half]
        sums_ref[3:4, :] = jnp.sum(gain_acc[...], axis=0, keepdims=True)
        sums_ref[4:5, :] = jnp.sum(gain_terms_ref[...], axis=0, keepdims=True)
        rows = in_acc.shape[0] // chips
        copies = []
        for a, (halves, keeps, sends) in enumerate(
            (
                (((out_acc, 0), (in_acc, 0)), keep_a, send_a),
                (((in_acc, cols), (in_acc, 2 * cols)), keep_b, send_b),
            )
        ):
            for slot in range(2 * chips):
                number = a * 2 * chips + slot
                where = pl.ds(pl.multiple_of(slots[number] * rows, rows), rows)
                other = slot_pair(a, slot, chips)
                for at, (source, start) in enumerate(halves):
                    low = start + other * half
                    bufs[a, slot, :, at * half : (at + 1) * half] = source[
                        where, low : low + half
                    ].astype(LOW)
            sent = pltpu.make_async_copy(bufs.at[a, pl.ds(chips, chips)], sends, sems.at[a, 0])
            kept = pltpu.make_async_copy(bufs.at[a, pl.ds(0, chips)], keeps, sems.at[a, 1])
            sent.start()
            kept.start()
            copies += [sent, kept]
        for copy in copies:
            copy.wait()


def slot_pair(group, slot, chips):
    return slot // chips if group == 0 else (slot // (chips // 2)) % 2


def mix_orders(links):
    return ["pair"] + links, [links[0], "pair"] + links[1:]


def conv_back(idx, slots, chips, own, other, edges, x, gain_terms, kept, in_weight, out_weight, far, taps, keeps, block):
    normed_mix, parts, conv_in, conv_out, mixed, c_edge = kept
    rows, width = own.shape
    half = far[0].shape[2]
    cols = 2 * half
    tile = TILE
    count = rows // tile

    def rowed(columns):
        return pl.BlockSpec((tile, columns), lambda i, s, t: (i, 0))

    def fixed(array):
        zeros = (0,) * array.ndim
        return pl.BlockSpec(array.shape, lambda i, s, t: zeros)

    lower = pl.BlockSpec((tile, width), lambda i, s, t: (jnp.minimum(i, count - 1), 0))
    upper = pl.BlockSpec((tile, width), lambda i, s, t: (jnp.maximum(i - count, 0), 0))
    any_spec = pl.BlockSpec(memory_space=pl.ANY)
    grad = jax.ShapeDtypeStruct((chips, width // chips, cols), LOW)
    return call(
        functools.partial(conv_back_body, block, count, chips),
        "conv_back",
        (2 * count,),
        [
            lower,
            upper,
            fixed(edges),
            rowed(width),
            fixed(gain_terms),
            rowed(width),
            rowed(cols),
            rowed(3 * cols),
            rowed(cols),
            rowed(cols),
            fixed(c_edge),
            pl.BlockSpec((3, width, half), lambda i, s, t: (0, 0, s[0])),
            pl.BlockSpec((half, width), lambda i, s, t: (s[0], 0)),
            *[fixed(piece) for piece in far],
            fixed(taps),
            rowed(keeps.shape[1]),
        ],
        [lower, upper, pl.BlockSpec((8, width), lambda i, s, t: (0, 0))] + [any_spec] * 4,
        [
            shape(rows, width),
            shape(rows, width),
            shape(8, width, F32),
        ]
        + [grad] * 4,
        [
            pltpu.VMEM((tile, width), LOW),
            pltpu.VMEM((edges.shape[0], cols), F32),
            pltpu.VMEM((tile, width), F32),
            pltpu.VMEM((tile, 3 * cols), LOW),
            pltpu.VMEM((width, 3 * cols), F32),
            pltpu.VMEM((width, cols), F32),
            pltpu.VMEM((3, 8, cols), F32),
            pltpu.VMEM((8, width), F32),
            pltpu.VMEM((2, 2 * chips, width // chips, cols), LOW),
            pltpu.SemaphoreType.DMA((2, 2)),
        ],
        scalars=2,
        mib=48,
    )(
        idx,
        slots,
        own,
        other,
        edges,
        x,
        gain_terms,
        normed_mix,
        mixed,
        parts,
        conv_in,
        conv_out,
        c_edge,
        in_weight,
        out_weight,
        *far,
        taps,
        keeps,
    )


def hidden_back_body(mine_ref, came_ref, x_ref, d_ref, gain_ref, out_ref):
    upstream = mine_ref[...].astype(F32) + came_ref[...].astype(F32)
    resid = x_ref[...].astype(F32)
    scale = lax.rsqrt(jnp.mean(resid * resid, axis=-1, keepdims=True) + EPS)
    out_ref[...] = d_ref[...] + norm_back(upstream, resid, scale, gain_ref[...])[0]


def hidden_back(mine, came, x, d_resid, gain):
    rows, width = x.shape
    plain = pl.BlockSpec((TILE // 2, width), lambda i: (i, 0))
    return call(
        hidden_back_body,
        "hidden_back",
        (2 * rows // TILE,),
        [plain] * 4 + [whole(gain)],
        plain,
        shape(rows, width, F32),
        scalars=0,
        mib=12,
    )(mine, came, x, d_resid, gain)


class Halving:
    def __init__(self, keep, order):
        self.terms = [keep]
        self.half = keep.shape[0]
        self.links = list(order)

    def start(self, send):
        self.terms.append(swap(send, self.links.pop(0)))

    def step(self, *after, first=None):
        self.half //= 2
        half = self.half
        terms = self.terms
        if after:
            terms = [tie(terms[0], *after)] + terms[1:]
        going = sum(term[half : 2 * half].astype(F32) for term in terms).astype(LOW)
        link = self.links.pop(0)
        self.terms.append(swap(going, link))
        if first is not None:
            first = first + tie(swap(first, link), self.terms[-1])
        return first

    def done(self):
        return sum(term[0].astype(F32) for term in self.terms)


def local(
    hidden,
    segments,
    cotangent,
    in_weight,
    out_weight,
    gate_weight,
    up_weight,
    down_weight,
    conv_weight,
    norm_mix,
    norm_ffn,
):
    groups, block, width = hidden.shape
    rows = groups * block
    size = lax.axis_size("seq")
    seq_index = lax.axis_index("seq")
    core = seq_index % 2
    chip = seq_index // 2
    pair = lax.axis_index("wshard")
    first_core = core == 0
    chips = size // 2
    links = [1 << bit for bit in range(chips.bit_length() - 1)]
    turned = [links[1], links[0]] + links[2:]
    half = out_weight.shape[0] // 2
    cols = 2 * half
    place = chip & 3
    idx = jnp.stack([core, place, pair]).astype(jnp.int32)

    def slots_of(*orders):
        masks = [mask for order in orders for mask in slot_masks(order)]
        return (chip ^ jnp.array(masks, jnp.int32)).astype(jnp.int32)

    weights = (gate_weight, up_weight, down_weight)

    def ordered(flag, mine, other, axis):
        return jnp.where(
            flag,
            jnp.concatenate([mine, other], axis=axis),
            jnp.concatenate([other, mine], axis=axis),
        )

    small = jnp.concatenate([conv_weight, norm_mix[None], norm_ffn[None]], axis=0)
    in_planes = jnp.transpose(in_weight, (1, 0, 2))
    depth = width // 4

    def piece(number):
        from_in = lax.dynamic_slice(in_planes, (0, number * depth, core * half), (3, depth, half))
        from_out = lax.dynamic_slice(out_weight, (core * half, number * depth), (half, depth))
        return jnp.concatenate([from_in, from_out[None]], axis=0)

    small_other = swap_pair(small)
    sent_zero = tie(piece(place), small)
    sent_three = piece(place ^ 3)
    piece_zero = swap_pair(sent_zero)
    piece_three = swap_pair(sent_three)
    piece_one = swap(piece_zero, 1)
    piece_two = swap(piece_zero, 2)
    far_weights = (piece_zero, piece_one, piece_two, piece_three)

    hidden, segments = lax.optimization_barrier((hidden, segments, sent_zero, sent_three))[:2]
    own = hidden.reshape(rows, width)
    other = swap_core(own)
    chip_hidden = jnp.concatenate([own, other], axis=0)
    cot = cotangent.reshape(rows, width)
    cot_far = swap_pair(jnp.concatenate([tie(cot, piece_zero), cot[:16]], axis=0))

    seg_low = segments.astype(LOW)
    seg_other = swap_core(seg_low)

    def with_seg(values, segs):
        return jnp.concatenate(
            [values, jnp.broadcast_to(segs[:, :, None], (groups, segs.shape[1], 128))], axis=2
        )

    def ends(values, segs):
        both = values.reshape(groups, block, width)
        return (
            with_seg(both[:, :2], segs[:, :2]),
            with_seg(both[:, block - 2 :], segs[:, block - 2 :]),
        )

    head, last = ends(own, seg_low)
    other_head, other_last = ends(other, seg_other)
    even = range(2, size, 2)
    forth = [(i - 2, i) for i in range(2, size)]
    back = [(i, i - 2) for i in range(2, size)]
    from_before = over_seq(jnp.where(first_core, other_last, last), forth)
    from_after = over_seq(jnp.where(first_core, head, other_head), back)

    def after_blocks(outside, own_head, near_head):
        return jnp.where(
            first_core, jnp.stack([near_head, outside]), jnp.stack([outside, own_head])
        )

    before = jnp.where(
        first_core, jnp.stack([from_before, last]), jnp.stack([other_last, from_before])
    )
    after = after_blocks(from_after, head, other_head)
    edges = jnp.concatenate([before, after], axis=0)
    edge_rows = edges[..., :width].reshape(8 * groups, width)
    edge_segs = edges[..., width]
    segs = jnp.stack([seg_low, seg_other])
    segs_ext = jnp.concatenate([edge_segs[:2], segs, edge_segs[2:]], axis=2)
    keeps = jnp.stack(
        [(segs_ext[:, :, at : at + block] == segs).astype(F32) for at in (1, 0, 3, 4)], axis=-1
    ).reshape(2 * rows, 4)

    gains = ordered(pair == 0, small[3:], small_other[3:], 1).astype(F32)
    gain_mix, gain_ffn = gains[:1], gains[1:]
    taps = jnp.concatenate(
        [lax.dynamic_slice_in_dim(part[:3], core * half, half, 1) for part in (small, small_other)],
        axis=1,
    ).astype(F32)

    normed_mix, parts, conv_in, conv_out, mixed, mix_own, mix_other, c_edge = conv_forward(
        idx, chip_hidden, edge_rows, in_planes, out_weight, far_weights, gain_mix, taps, keeps, block
    )
    mix_to_own = swap_core(mix_other)
    mix_to_other = swap_core(mix_own)
    own_x, resid_two = second_norm(
        tie(chip_hidden, cot_far), mix_own, mix_to_own, gain_ffn, 0, True
    )
    far_x = swap_pair(own_x)
    other_x = second_norm(
        tie(chip_hidden, own_x), mix_other, mix_to_other, gain_ffn, 1, False
    )[0]

    cot_other = swap_core(tie(cot, piece_zero))
    cot_far = tie(cot_far, own_x)[:rows]
    cot_diag = swap_core(cot_far)
    total = 4 * rows
    act, d_gate, d_up, term_own, term_other, d_own, d_other = feed_forward(
        idx, [own_x, other_x], [cot, cot_other], weights, total, 0, ()
    )
    diag_x = swap_core(tie(far_x, d_own))
    near_d = swap_core(d_other)
    near_term = swap_core(term_other)
    act, d_gate, d_up, term_far, term_diag, d_far, d_diag = feed_forward(
        idx,
        [far_x, diag_x],
        [cot_far, cot_diag],
        weights,
        total,
        2 * rows // TILE,
        (act, d_gate, d_up),
    )
    d_diag_came = swap_core(d_diag)
    down_send, down_keep = weight_grads(
        slots_of(links), chips, [cot, cot_other, cot_far, cot_diag], [act]
    )
    sum_down = Halving(down_keep, links)
    sum_down.start(down_send)
    home = swap_pair(
        (d_far.astype(F32) + tie(d_diag_came, down_send).astype(F32)).astype(LOW)
    )
    term_home = swap_pair(
        (term_far.astype(F32) + swap_core(tie(term_diag, down_send)).astype(F32)).astype(LOW)
    )
    xs = [own_x, other_x, far_x, diag_x]
    gate_send, gate_keep = weight_grads(slots_of(turned), chips, xs, [tie(d_gate, down_send)])
    up_send, up_keep = weight_grads(slots_of(links), chips, xs, [tie(d_up, gate_send)])

    d_resid, d_low, gain_ffn_terms = resid_back(
        d_own, near_d, home, tie(resid_two, up_send), cot, gain_ffn
    )
    d_near = swap_core(d_low)
    d_head = d_low.reshape(groups, block, width)[:, :2]
    d_after = jnp.where(
        first_core,
        over_seq(d_head, [(i, i - 2) for i in even]),
        over_seq(d_head, [(i, i - 1) for i in even]),
    )
    sum_gate = Halving(gate_keep, turned)
    sum_gate.start(tie(gate_send, d_head))
    sum_up = Halving(up_keep, links)
    sum_up.start(tie(up_send, d_head))
    d_edges = after_blocks(
        d_after, d_head, d_near.reshape(groups, block, width)[:, :2]
    ).reshape(4 * groups, width)
    sum_down.step(d_low)
    orders = mix_orders(links)
    slots_mix = slots_of(
        *[[0 if link == "pair" else link for link in order] for order in orders]
    )
    d_normed_own, d_normed_other, sums, send_a, keep_a, send_b, keep_b = conv_back(
        idx,
        slots_mix,
        chips,
        d_low,
        d_near,
        d_edges,
        chip_hidden,
        gain_ffn_terms,
        (normed_mix, parts, conv_in, conv_out, mixed, c_edge),
        in_planes,
        out_weight,
        far_weights,
        taps,
        keeps,
        block,
    )
    sum_a = Halving(keep_a, orders[0])
    sum_b = Halving(keep_b, orders[1])
    sum_a.start(send_a)
    sum_b.start(send_b)
    sums = sums + tie(swap_pair(sums), sum_a.terms[-1])
    d_normed_came = swap_core(d_normed_other)
    sum_gate.step(send_a)
    sum_up.step(send_a)
    sum_down.step(send_a)
    grad_hidden = hidden_back(d_normed_own, d_normed_came, own, d_resid, gain_mix)
    for reduction in (sum_down, sum_gate, sum_up):
        while reduction.links:
            reduction.step(grad_hidden)
    while sum_a.links:
        sums = sum_a.step(first=sums)
        sum_b.step()
    sums = sums + swap_core(sums)
    half_width = norm_mix.shape[0]
    sums = lax.dynamic_slice_in_dim(sums, pair * half_width, half_width, 1)

    block_out = (
        resid_two
        + (term_own.astype(F32) + near_term.astype(F32) + tie(term_home, send_a).astype(F32))
    ).astype(LOW)

    part_rows = width // size

    def finish(reductions):
        total = jnp.concatenate([reduction.done() for reduction in reductions], axis=1)
        total = total.reshape(2, part_rows, -1)
        came = swap_core(
            jnp.where(first_core, total[1], total[0]).astype(LOW)
        ).astype(F32)
        mine = jnp.where(first_core, total[0], total[1])
        each = mine.shape[1] // (3 if len(reductions) == 3 else 4)
        return [
            ordered(first_core, mine[:, at : at + each], came[:, at : at + each], 1)
            for at in range(0, mine.shape[1], each)
        ]

    out_down, out_gate, out_up = finish([sum_down, sum_gate, sum_up])
    out_out, out_b, out_c, out_x = finish([sum_a, sum_b])
    return (
        block_out.reshape(groups, block, width),
        grad_hidden.reshape(groups, block, width),
        jnp.stack([out_b, out_c, out_x], axis=1),
        out_out.T,
        out_gate,
        out_up,
        out_down.T,
        sums[:3],
        sums[3],
        sums[4],
    )


def solution(mesh):
    return jax.shard_map(
        local,
        mesh=mesh,
        in_specs=(
            P("wshard", "seq", None),
            P("wshard", "seq"),
            P("wshard", "seq", None),
            P(None, None, "wshard"),
            P("wshard", None),
            P(None, "wshard"),
            P(None, "wshard"),
            P("wshard", None),
            P(None, "wshard"),
            P("wshard"),
            P("wshard"),
        ),
        out_specs=(
            P("wshard", "seq", None),
            P("wshard", "seq", None),
            P("seq", None, "wshard"),
            P("wshard", "seq"),
            P("seq", "wshard"),
            P("seq", "wshard"),
            P("wshard", "seq"),
            P(None, "wshard"),
            P("wshard"),
            P("wshard"),
        ),
        check_vma=False,
    )
```

```python
import functools

import jax
import jax.numpy as jnp
from jax import lax
from jax.experimental import pallas as pl
from jax.experimental.pallas import tpu as pltpu
from jax.sharding import PartitionSpec as P

EPS = 1e-05
LOW = jnp.bfloat16
F32 = jnp.float32
TILE = 256
NT = (((1,), (1,)), ((), ()))
TN = (((0,), (0,)), ((), ()))


def over_seq(block, route):
    return lax.ppermute(block, "seq", route)


def swap_seq(block, mask):
    return over_seq(block, [(i, i ^ mask) for i in range(lax.axis_size("seq"))])


def swap_core(block):
    return swap_seq(block, 1)


def swap_pair(block):
    return lax.ppermute(block, "wshard", [(0, 1), (1, 0)])


def swap(block, link):
    return swap_pair(block) if link == "pair" else swap_seq(block, 2 * link)


def in_hbm(array):
    return pltpu.with_memory_space_constraint(array, pltpu.HBM)


def tie(value, *after):
    return lax.optimization_barrier((value,) + after)[0]


def dot(left, right):
    return jnp.dot(left, right, preferred_element_type=F32)


def dot_nt(left, right):
    return lax.dot_general(left, right, NT, preferred_element_type=F32)


def dot_tn(left, right):
    return lax.dot_general(left, right, TN, preferred_element_type=F32)


def call(
    body, name, grid, in_specs, out_specs, out_shape, scratch=(), scalars=1, aliases=None, mib=36
):
    return pl.pallas_call(
        body,
        grid_spec=pltpu.PrefetchScalarGridSpec(
            num_scalar_prefetch=scalars,
            grid=grid,
            in_specs=in_specs,
            out_specs=out_specs,
            scratch_shapes=list(scratch),
        ),
        out_shape=out_shape,
        input_output_aliases=aliases or {},
        compiler_params=pltpu.CompilerParams(vmem_limit_bytes=mib * 2**20),
        cost_estimate=pl.CostEstimate(flops=1000, bytes_accessed=1000, transcendentals=0),
        name=name,
    )


def shape(rows, cols, kind=LOW):
    return jax.ShapeDtypeStruct((rows, cols), kind)


def whole(array):
    zeros = (0,) * array.ndim
    return pl.BlockSpec(array.shape, lambda *_: zeros)


def normed(values, gain):
    wide = values.astype(F32)
    scale = lax.rsqrt(jnp.mean(wide * wide, axis=-1, keepdims=True) + EPS)
    return wide * scale * gain, scale


def piece_columns(place, j, depth):
    return pl.ds(pl.multiple_of((place ^ j) * depth, depth), depth)


def conv_forward_body(
    block,
    idx,
    own_ref,
    other_ref,
    edge_ref,
    in_ref,
    out_ref,
    r0,
    r1,
    r2,
    r3,
    gain_ref,
    taps_ref,
    keep_ref,
    normed_ref,
    parts_ref,
    conv_in_ref,
    conv_out_ref,
    mixed_ref,
    own_mix_ref,
    other_mix_ref,
    c_edge_ref,
    nx,
    edge_in,
    acc,
):
    step = pl.program_id(0)
    place = idx[1]
    far = (r0, r1, r2, r3)
    half = r0.shape[1]
    depth = r0.shape[0] // 4
    cols = 2 * half
    gain = gain_ref[...]

    def project(load, j):
        mine = dot(load(slice(None)), in_ref[j])
        other = None
        for p in range(4):
            term = dot(load(piece_columns(place, p, depth)), far[p][j * depth : (j + 1) * depth])
            other = term if other is None else other + term
        return jnp.concatenate([mine, other], axis=1)

    @pl.when(step == 0)
    def _():
        count = edge_ref.shape[0]
        nx[:count] = normed(edge_ref[...], gain)[0].astype(LOW)

        def load(columns):
            return nx[:count, columns]

        before = count // 2
        edge_b, edge_c, edge_x = (project(load, j) for j in range(3))
        edge_in[...] = (edge_b[:before] * edge_x[:before]).astype(LOW).astype(F32)
        c_edge_ref[...] = edge_c[before:]

    count = pl.num_programs(0) // 2
    x = jnp.where(step < count, own_ref[...], other_ref[...])
    nx[...] = normed(x, gain)[0].astype(LOW)
    normed_ref[...] = nx[...]

    def load(columns):
        return nx[:, columns]

    b_part, c_part, x_part = (project(load, j) for j in range(3))
    parts_ref[:, :cols] = b_part.astype(LOW)
    parts_ref[:, cols : 2 * cols] = c_part.astype(LOW)
    parts_ref[:, 2 * cols :] = x_part.astype(LOW)
    low_in = (b_part * x_part).astype(LOW)
    conv_in_ref[...] = low_in
    conv_in = low_in.astype(F32)
    groups = own_ref.shape[0] // block
    row = lax.broadcasted_iota(jnp.int32, (block, cols), 0)
    for g in range(groups):
        span = slice(g * block, (g + 1) * block)
        here = conv_in[span]
        base = step * 2 * groups + 2 * g
        two_before = edge_in[pl.ds(base, 1), :]
        one_before = edge_in[pl.ds(base + 1, 1), :]
        lag_one = jnp.where(row == 0, one_before, pltpu.roll(here, 1, 0))
        lag_two = jnp.where(
            row == 0, two_before, jnp.where(row == 1, one_before, pltpu.roll(here, 2, 0))
        )
        conv_out = (
            taps_ref[2:3, :] * here
            + taps_ref[1:2, :] * (keep_ref[span, 0:1] * lag_one)
            + taps_ref[0:1, :] * (keep_ref[span, 1:2] * lag_two)
        )
        conv_out_ref[span, :] = conv_out.astype(LOW)
        mixed_ref[span, :] = (c_part[span] * conv_out).astype(LOW)
    mixed = mixed_ref[...]
    acc[...] = dot(mixed[:, :half], out_ref[...])
    for p in range(4):
        where = piece_columns(place, p, depth)
        acc[:, where] += dot(mixed[:, half:], far[p][3 * depth : 4 * depth])
    mix = acc[...].astype(LOW)

    @pl.when(step < count)
    def _():
        own_mix_ref[...] = mix

    @pl.when(step >= count)
    def _():
        other_mix_ref[...] = mix


def conv_forward(idx, own, other, edges, in_weight, out_weight, far, gain, taps, keeps, block):
    total, width = 2 * own.shape[0], own.shape[1]
    rows = TILE
    half = far[0].shape[1]
    cols = 2 * half

    def rowed(columns):
        return pl.BlockSpec((rows, columns), lambda i, s: (i, 0))

    before = edges.shape[0] // 2
    count = total // rows // 2
    return call(
        functools.partial(conv_forward_body, block),
        "conv_forward",
        (total // rows,),
        [
            pl.BlockSpec((rows, width), lambda i, s: (jnp.minimum(i, count - 1), 0)),
            pl.BlockSpec((rows, width), lambda i, s: (jnp.maximum(i - count, 0), 0)),
            whole(edges),
            pl.BlockSpec((3, width, half), lambda i, s: (0, 0, s[0])),
            pl.BlockSpec((half, width), lambda i, s: (s[0], 0)),
            *[whole(piece) for piece in far],
            whole(gain),
            whole(taps),
            rowed(keeps.shape[1]),
        ],
        [
            rowed(width),
            rowed(3 * cols),
            rowed(cols),
            rowed(cols),
            rowed(cols),
            pl.BlockSpec((rows, width), lambda i, s: (jnp.minimum(i, count - 1), 0)),
            pl.BlockSpec((rows, width), lambda i, s: (jnp.maximum(i - count, 0), 0)),
            pl.BlockSpec((before, cols), lambda i, s: (0, 0)),
        ],
        [
            pltpu.HBM((total, width), LOW),
            pltpu.HBM((total, 3 * cols), LOW),
            pltpu.HBM((total, cols), LOW),
            pltpu.HBM((total, cols), LOW),
            pltpu.HBM((total, cols), LOW),
            shape(total // 2, width),
            shape(total // 2, width),
            shape(before, cols, F32),
        ],
        [
            pltpu.VMEM((rows, width), LOW),
            pltpu.VMEM((before, cols), F32),
            pltpu.VMEM((rows, width), F32),
        ],
    )(idx, own, other, edges, in_hbm(in_weight), in_hbm(out_weight), *far, gain, taps, keeps)


def second_norm_body(x_ref, mine_ref, came_ref, gain_ref, low_ref, *resid_ref):
    two = x_ref[...].astype(F32) + (mine_ref[...].astype(F32) + came_ref[...].astype(F32))
    low_ref[...] = normed(two, gain_ref[...])[0].astype(LOW)
    for ref in resid_ref:
        ref[...] = two


def second_norm(x, mine, came, gain, keep):
    rows, width = mine.shape
    tile = rows // 4

    plain = pl.BlockSpec((tile, width), lambda i: (i, 0))

    return call(
        second_norm_body,
        "second_norm",
        (4,),
        [plain] * 3 + [whole(gain)],
        [plain] * (1 + keep),
        [pltpu.HBM((rows, width), LOW), pltpu.HBM((rows, width), F32)][: 1 + keep],
        scalars=0,
        mib=12,
    )(x, mine, came, gain)


def feed_forward_body(count, held, idx, *refs):
    x_refs, ct_refs = refs[:2], refs[2:4]
    gate_ref, up_ref, down_ref = refs[4:7]
    refs = refs[7 + held :]
    act_ref, d_gate_ref, d_up_ref, term_a, term_b, d_a, d_b = refs
    step = pl.program_id(0)
    first = step < count
    x = jnp.where(first, x_refs[0][...], x_refs[1][...])
    upstream = jnp.where(first, ct_refs[0][...], ct_refs[1][...])
    gate = dot(x, gate_ref[...])
    up_value = dot(x, up_ref[...])
    d_act = dot_nt(upstream, down_ref[...])
    sigma = jax.nn.sigmoid(gate)
    silu_gate = gate * sigma
    act = (silu_gate * up_value).astype(LOW)
    d_gate = (d_act * up_value * (sigma * (1.0 + gate * (1.0 - sigma)))).astype(LOW)
    d_up = (d_act * silu_gate).astype(LOW)
    act_ref[...] = act
    d_gate_ref[...] = d_gate
    d_up_ref[...] = d_up
    d_normed = (dot_nt(d_gate, gate_ref[...]) + dot_nt(d_up, up_ref[...])).astype(LOW)
    term = dot(act, down_ref[...]).astype(LOW)

    @pl.when(first)
    def _():
        d_a[...] = d_normed
        term_a[...] = term

    @pl.when(step >= count)
    def _():
        d_b[...] = d_normed
        term_b[...] = term


def feed_forward(idx, xs, cts, weights, total, start, held):
    gate, up, down = weights
    rows, width = xs[0].shape
    units = gate.shape[1] // 2
    count = rows // TILE

    def rowed(index):
        return pl.BlockSpec((TILE, width), index)

    def lower(i, s):
        return (jnp.minimum(i, count - 1), 0)

    def upper(i, s):
        return (jnp.maximum(i - count, 0), 0)

    any_spec = pl.BlockSpec(memory_space=pl.ANY)
    unit_spec = pl.BlockSpec((TILE, units), lambda i, s: (i + start, 0))
    columns = pl.BlockSpec((width, units), lambda i, s: (0, s[0]))
    return call(
        functools.partial(feed_forward_body, count, len(held)),
        "feed_forward",
        (2 * count,),
        [rowed(lower), rowed(upper)] * 2
        + [columns, columns, pl.BlockSpec((units, width), lambda i, s: (s[0], 0))]
        + [any_spec] * len(held),
        [unit_spec] * 3 + [rowed(lower), rowed(upper)] * 2,
        [pltpu.VMEM((total, units), LOW)] * 3 + [shape(rows, width)] * 4,
        aliases={8 + k: k for k in range(len(held))},
        mib=30,
    )(idx, *[in_hbm(x) for x in (*xs, *cts)], gate, up, down, *held)


def slot_masks(order):
    masks = [0]
    for link in reversed(order):
        masks = masks + [mask ^ link for mask in masks]
    return masks


def grads_body(pieces, cut, chips, part, held, slots, *refs):
    x_hbm, refs = refs[:pieces], refs[pieces:]
    y_hbm, refs = refs[0], refs[1 + held :]
    outs, refs = refs[:4], refs[4:]
    x_buf, y_buf, acc, low_buf, high_buf, x_sems, y_sems, out_sems = refs
    depth = x_buf.shape[1]
    copies = []
    for k in range(pieces):
        from_y = y_hbm.at[pl.ds(k * depth, depth)]
        copies.append(
            pltpu.make_async_copy(x_hbm[k].at[pl.ds(0, depth)], x_buf.at[k], x_sems.at[k])
        )
        copies.append(pltpu.make_async_copy(from_y, y_buf.at[k], y_sems.at[k]))
    for copy in copies:
        copy.start()
    for copy in copies:
        copy.wait()
    for k in range(pieces):
        term = dot_tn(x_buf[k], y_buf[k])
        if k == 0:
            acc[...] = term
        else:
            acc[...] += term
    rows = acc.shape[0] // chips
    half = chips // 2
    copies = []
    for a, (buf, columns) in enumerate(
        ((low_buf, slice(0, cut)), (high_buf, slice(cut, acc.shape[1])))
    ):
        for slot in range(chips):
            where = pl.ds(pl.multiple_of(slots[a * chips + slot] * rows, rows), rows)
            buf[slot] = acc[where, columns].astype(LOW)
        count = buf.shape[2]
        for at, start in enumerate((half, 0)):
            copies.append(
                pltpu.make_async_copy(
                    buf.at[pl.ds(start, half)],
                    outs[2 * a + at].at[:, :, pl.ds(part * count, count)],
                    out_sems.at[a, at],
                )
            )
            copies[-1].start()
    for copy in copies:
        copy.wait()


def weight_grads(slots, chips, cut, xs, y, part=0, parts=1, held=()):
    depth, width = xs[0].shape
    units = y.shape[1]
    pieces = len(xs)
    rows = width // chips
    any_spec = pl.BlockSpec(memory_space=pl.ANY)
    counts = (cut, cut, units - cut, units - cut)
    return call(
        functools.partial(grads_body, pieces, cut, chips, part, len(held)),
        "weight_grads",
        (),
        [any_spec] * (pieces + 1 + len(held)),
        [any_spec] * 4,
        [pltpu.HBM((chips // 2, rows, parts * count), LOW) for count in counts],
        [
            pltpu.VMEM((pieces, depth, width), LOW),
            pltpu.VMEM((pieces, depth, units), LOW),
            pltpu.VMEM((width, units), F32),
            pltpu.VMEM((chips, rows, cut), LOW),
            pltpu.VMEM((chips, rows, units - cut), LOW),
            pltpu.SemaphoreType.DMA((pieces,)),
            pltpu.SemaphoreType.DMA((pieces,)),
            pltpu.SemaphoreType.DMA((2, 2)),
        ],
        aliases={2 + pieces + k: k for k in range(len(held))},
        mib=26,
    )(slots, *[in_hbm(x) for x in xs], y, *held)


def norm_back(upstream, values, scale, gain):
    scaled = values * scale
    weighted = upstream * gain
    inner = jnp.mean(weighted * scaled, axis=-1, keepdims=True)
    return scale * (weighted - scaled * inner), upstream * scaled


def resid_back_body(mine_ref, near_ref, far_ref, two_ref, cot_ref, gain_ref, d_ref, low_ref, sum_ref):
    step = pl.program_id(0)
    upstream = mine_ref[...].astype(F32) + near_ref[...].astype(F32) + far_ref[...].astype(F32)
    two = two_ref[...]
    scale = lax.rsqrt(jnp.mean(two * two, axis=-1, keepdims=True) + EPS)
    back, terms = norm_back(upstream, two, scale, gain_ref[...])
    d_resid = cot_ref[...].astype(F32) + back
    d_ref[...] = d_resid
    low_ref[...] = d_resid.astype(LOW)
    part = jnp.sum(terms.reshape(-1, 8, terms.shape[1]), axis=0)

    @pl.when(step == 0)
    def _():
        sum_ref[...] = part

    @pl.when(step > 0)
    def _():
        sum_ref[...] += part


def resid_back(mine, near, far, two, cot, gain):
    rows, width = two.shape

    def plain(kind=None):
        return pl.BlockSpec((TILE, width), lambda i: (i, 0))

    return call(
        resid_back_body,
        "resid_back",
        (rows // TILE,),
        [plain()] * 5 + [whole(gain)],
        [plain(), plain(), pl.BlockSpec((8, width), lambda i: (0, 0))],
        [pltpu.HBM((rows, width), F32), pltpu.HBM((rows, width), LOW), shape(8, width, F32)],
        scalars=0,
        mib=16,
    )(mine, near, far, two, cot, gain)


def conv_back_body(
    block,
    count,
    chips,
    idx,
    slots,
    own_ref,
    other_ref,
    edge_ref,
    gain_terms_ref,
    normed_ref,
    mixed_ref,
    parts_ref,
    conv_in_ref,
    conv_out_ref,
    c_edge_ref,
    out_ref,
    r0,
    r1,
    r2,
    r3,
    taps_ref,
    keep_ref,
    d_proj,
    sums_ref,
    send_a,
    keep_a,
    send_b,
    keep_b,
    held,
    edge_d,
    in_acc,
    out_acc,
    taps_acc,
    bufs,
    sems,
):
    step = pl.program_id(0)
    place = idx[1]
    far = (r0, r1, r2, r3)
    half = r0.shape[1]
    depth = r0.shape[0] // 4
    cols = 2 * half

    def back_out(load):
        mine = dot_nt(load(slice(None)), out_ref[...])
        other = None
        for p in range(4):
            term = dot_nt(load(piece_columns(place, p, depth)), far[p][3 * depth : 4 * depth])
            other = term if other is None else other + term
        return jnp.concatenate([mine, other], axis=1)

    @pl.when(step == 0)
    def _():
        edge_d[...] = back_out(lambda columns: edge_ref[:, columns]) * c_edge_ref[...]
        in_acc[...] = jnp.zeros_like(in_acc)
        out_acc[...] = jnp.zeros_like(out_acc)
        taps_acc[...] = jnp.zeros_like(taps_acc)

    held[...] = jnp.where(step < count, own_ref[...], other_ref[...])
    d_mixed = back_out(lambda columns: held[:, columns])
    d_conv = d_mixed * parts_ref[:, cols : 2 * cols].astype(F32)
    d_proj[:, cols : 2 * cols] = (d_mixed * conv_out_ref[...].astype(F32)).astype(LOW)
    groups = own_ref.shape[0] // block
    row = lax.broadcasted_iota(jnp.int32, (block, cols), 0)
    for g in range(groups):
        span = slice(g * block, (g + 1) * block)
        here = d_conv[span]
        base = step * 2 * groups + 2 * g
        after_one = edge_d[pl.ds(base, 1), :]
        after_two = edge_d[pl.ds(base + 1, 1), :]
        next_one = jnp.where(row == block - 1, after_one, pltpu.roll(here, block - 1, 0))
        next_two = jnp.where(
            row == block - 1,
            after_two,
            jnp.where(row == block - 2, after_one, pltpu.roll(here, block - 2, 0)),
        )
        next_one = keep_ref[span, 2:3] * next_one
        next_two = keep_ref[span, 3:4] * next_two
        d_in = taps_ref[2:3, :] * here + taps_ref[1:2, :] * next_one + taps_ref[0:1, :] * next_two
        conv_in = conv_in_ref[span, :].astype(F32)
        for k, term in enumerate((next_two, next_one, here)):
            taps_acc[k] += jnp.sum((term * conv_in).reshape(-1, 8, cols), axis=0)
        d_proj[span, :cols] = (d_in * parts_ref[span, 2 * cols :].astype(F32)).astype(LOW)
        d_proj[span, 2 * cols :] = (d_in * parts_ref[span, :cols].astype(F32)).astype(LOW)
    out_acc[...] += dot_tn(held[...], mixed_ref[...])
    in_acc[...] += dot_tn(normed_ref[...], d_proj[...])
    @pl.when(step == 2 * count - 1)
    def _():
        sums_ref[...] = jnp.zeros_like(sums_ref)
        for k in range(3):
            line = jnp.sum(taps_acc[k], axis=0, keepdims=True)
            for part in range(2):
                side = idx[2] if part == 0 else 1 - idx[2]
                at = pl.multiple_of((2 * side + idx[0]) * half, 128)
                sums_ref[k : k + 1, pl.ds(at, half)] = line[:, part * half : (part + 1) * half]
        sums_ref[4:5, :] = jnp.sum(gain_terms_ref[...], axis=0, keepdims=True)
        rows = in_acc.shape[0] // chips
        copies = []
        for a, (halves, keeps, sends) in enumerate(
            (
                (((out_acc, 0), (in_acc, 0)), keep_a, send_a),
                (((in_acc, cols), (in_acc, 2 * cols)), keep_b, send_b),
            )
        ):
            for slot in range(2 * chips):
                number = a * 2 * chips + slot
                where = pl.ds(pl.multiple_of(slots[number] * rows, rows), rows)
                other = slot_pair(a, slot, chips)
                for at, (source, start) in enumerate(halves):
                    low = start + other * half
                    bufs[a, slot, :, at * half : (at + 1) * half] = source[
                        where, low : low + half
                    ].astype(LOW)
            sent = pltpu.make_async_copy(bufs.at[a, pl.ds(chips, chips)], sends, sems.at[a, 0])
            kept = pltpu.make_async_copy(bufs.at[a, pl.ds(0, chips)], keeps, sems.at[a, 1])
            sent.start()
            kept.start()
            copies += [sent, kept]
        for copy in copies:
            copy.wait()


def slot_pair(group, slot, chips):
    return slot // chips if group == 0 else (slot // (chips // 2)) % 2


def mix_orders(links):
    return ["pair"] + links, [links[0], "pair"] + links[1:]


def conv_back(idx, slots, chips, own, other, edges, gain_terms, kept, out_weight, far, taps, keeps, block):
    normed_mix, parts, conv_in, conv_out, mixed, c_edge = kept
    rows, width = own.shape
    half = far[0].shape[1]
    cols = 2 * half
    tile = TILE
    count = rows // tile

    def rowed(columns):
        return pl.BlockSpec((tile, columns), lambda i, s, t: (i, 0))

    def fixed(array):
        zeros = (0,) * array.ndim
        return pl.BlockSpec(array.shape, lambda i, s, t: zeros)

    lower = pl.BlockSpec((tile, width), lambda i, s, t: (jnp.minimum(i, count - 1), 0))
    upper = pl.BlockSpec((tile, width), lambda i, s, t: (jnp.maximum(i - count, 0), 0))
    any_spec = pl.BlockSpec(memory_space=pl.ANY)
    grad = pltpu.HBM((chips, width // chips, cols), LOW)
    return call(
        functools.partial(conv_back_body, block, count, chips),
        "conv_back",
        (2 * count,),
        [
            lower,
            upper,
            fixed(edges),
            fixed(gain_terms),
            rowed(width),
            rowed(cols),
            rowed(3 * cols),
            rowed(cols),
            rowed(cols),
            fixed(c_edge),
            pl.BlockSpec((half, width), lambda i, s, t: (s[0], 0)),
            *[fixed(piece) for piece in far],
            fixed(taps),
            rowed(keeps.shape[1]),
        ],
        [rowed(3 * cols), pl.BlockSpec((8, width), lambda i, s, t: (0, 0))] + [any_spec] * 4,
        [
            pltpu.HBM((2 * rows, 3 * cols), LOW),
            shape(8, width, F32),
        ]
        + [grad] * 4,
        [
            pltpu.VMEM((tile, width), LOW),
            pltpu.VMEM((edges.shape[0], cols), F32),
            pltpu.VMEM((width, 3 * cols), F32),
            pltpu.VMEM((width, cols), F32),
            pltpu.VMEM((3, 8, cols), F32),
            pltpu.VMEM((2, 2 * chips, width // chips, cols), LOW),
            pltpu.SemaphoreType.DMA((2, 2)),
        ],
        scalars=2,
        mib=48,
    )(
        idx,
        slots,
        in_hbm(own),
        in_hbm(other),
        edges,
        gain_terms,
        in_hbm(normed_mix),
        in_hbm(mixed),
        in_hbm(parts),
        in_hbm(conv_in),
        in_hbm(conv_out),
        c_edge,
        in_hbm(out_weight),
        *far,
        taps,
        keeps,
    )


def mix_back_body(count, idx, own_x_ref, other_x_ref, d_proj, in_ref, r0, r1, r2, r3, start_ref, own_ref, other_ref, sums_ref, acc, gain_acc):
    step = pl.program_id(0)
    place = idx[1]
    far = (r0, r1, r2, r3)
    half = r0.shape[1]
    depth = r0.shape[0] // 4
    cols = 2 * half

    @pl.when(step == 0)
    def _():
        gain_acc[...] = jnp.zeros_like(gain_acc)

    total = None
    for j in range(3):
        term = dot_nt(d_proj[:, j * cols : j * cols + half], in_ref[j])
        total = term if total is None else total + term
    acc[...] = total
    for p in range(4):
        where = piece_columns(place, p, depth)
        total = None
        for j in range(3):
            term = dot_nt(d_proj[:, j * cols + half : (j + 1) * cols], far[p][j * depth : (j + 1) * depth])
            total = term if total is None else total + term
        acc[:, where] += total
    wide = jnp.where(step < count, own_x_ref[...], other_x_ref[...]).astype(F32)
    scale = lax.rsqrt(jnp.mean(wide * wide, axis=-1, keepdims=True) + EPS)
    terms = acc[...] * (wide * scale)
    gain_acc[...] += jnp.sum(terms.reshape(-1, 8, terms.shape[1]), axis=0)

    @pl.when(step < count)
    def _():
        own_ref[...] = acc[...].astype(LOW)

    @pl.when(step >= count)
    def _():
        other_ref[...] = acc[...].astype(LOW)

    @pl.when(step == 2 * count - 1)
    def _():
        sums_ref[...] = start_ref[...]
        sums_ref[3:4, :] = jnp.sum(gain_acc[...], axis=0, keepdims=True)


def mix_back(idx, own, other, d_proj, in_weight, far, start):
    total, width = 2 * own.shape[0], own.shape[1]
    half = far[0].shape[1]
    count = total // TILE // 2

    def rowed(columns):
        return pl.BlockSpec((TILE, columns), lambda i, s: (i, 0))

    return call(
        functools.partial(mix_back_body, count),
        "mix_back",
        (2 * count,),
        [
            pl.BlockSpec((TILE, width), lambda i, s: (jnp.minimum(i, count - 1), 0)),
            pl.BlockSpec((TILE, width), lambda i, s: (jnp.maximum(i - count, 0), 0)),
            rowed(d_proj.shape[1]),
            pl.BlockSpec((3, width, half), lambda i, s: (0, 0, s[0])),
            *[whole(piece) for piece in far],
            whole(start),
        ],
        [
            pl.BlockSpec((TILE, width), lambda i, s: (jnp.minimum(i, count - 1), 0)),
            pl.BlockSpec((TILE, width), lambda i, s: (jnp.maximum(i - count, 0), 0)),
            pl.BlockSpec((8, width), lambda i, s: (0, 0)),
        ],
        [shape(total // 2, width), shape(total // 2, width), shape(8, width, F32)],
        [pltpu.VMEM((TILE, width), F32), pltpu.VMEM((8, width), F32)],
    )(idx, own, other, d_proj, in_hbm(in_weight), *far, start)


def hidden_back_body(mine_ref, came_ref, x_ref, d_ref, gain_ref, out_ref):
    upstream = mine_ref[...].astype(F32) + came_ref[...].astype(F32)
    resid = x_ref[...].astype(F32)
    scale = lax.rsqrt(jnp.mean(resid * resid, axis=-1, keepdims=True) + EPS)
    out_ref[...] = d_ref[...] + norm_back(upstream, resid, scale, gain_ref[...])[0]


def hidden_back(mine, came, x, d_resid, gain):
    rows, width = x.shape
    plain = pl.BlockSpec((TILE // 2, width), lambda i: (i, 0))
    return call(
        hidden_back_body,
        "hidden_back",
        (2 * rows // TILE,),
        [plain] * 4 + [whole(gain)],
        plain,
        shape(rows, width, F32),
        scalars=0,
        mib=12,
    )(mine, came, x, d_resid, gain)


def add_up_body(*refs):
    total = refs[0][...].astype(F32)
    for ref in refs[1:-1]:
        total = total + ref[...].astype(F32)
    refs[-1][...] = total.astype(LOW)


def add_up(*arrays):
    rows, width = arrays[0].shape
    tile = TILE // 2
    plain = pl.BlockSpec((tile, width), lambda i: (i, 0))
    return call(
        add_up_body,
        "add_up",
        (rows // tile,),
        [plain] * len(arrays),
        plain,
        pltpu.HBM((rows, width), LOW),
        scalars=0,
        mib=12,
    )(*arrays)


def sum_slots_body(offsets, spans, *refs):
    ins, out = refs[: len(offsets)], refs[len(offsets)]
    for low, high in spans:
        total = None
        for ref, at in zip(ins, offsets):
            if at <= low and high <= at + ref.shape[2]:
                term = ref[:, :, low - at : high - at].astype(F32)
                total = term if total is None else total + term
        out[:, :, low:high] = total.astype(out.dtype)


def sum_slots(inputs, spans, half):
    rows = inputs[0][0].shape[1]
    width = spans[-1][1]
    tile = max(rows // 2, 16)
    return call(
        functools.partial(sum_slots_body, [at for _, at in inputs], spans),
        "sum_slots",
        (rows // tile,),
        [
            pl.BlockSpec((half, tile, array.shape[2]), lambda i: (1, i, 0))
            for array, _ in inputs
        ],
        pl.BlockSpec((half, tile, width), lambda i: (0, i, 0)),
        pltpu.HBM((half, rows, width), LOW),
        scalars=0,
        mib=16,
    )(*[array for array, _ in inputs])


def last_sum_body(offsets, spans, idx, *refs):
    ins, (mine, send) = refs[: len(offsets)], refs[len(offsets) :]
    step = pl.program_id(0)
    for low, high in spans:
        total = None
        for ref, at in zip(ins, offsets):
            if at <= low and high <= at + ref.shape[2]:
                term = ref[0, :, low - at : high - at].astype(F32)
                total = term if total is None else total + term

        @pl.when(step == 0)
        def _():
            mine[:, low:high] = total

        @pl.when(step == 1)
        def _():
            send[:, low:high] = total.astype(LOW)


def last_sum(idx, inputs, spans):
    rows = inputs[0][0].shape[1] // 2
    width = spans[-1][1]
    out = pl.BlockSpec((rows, width), lambda i, s: (0, 0))
    return call(
        functools.partial(last_sum_body, [at for _, at in inputs], spans),
        "last_sum",
        (2,),
        [
            pl.BlockSpec((1, rows, array.shape[2]), lambda i, s: (0, (i + s[0]) % 2, 0))
            for array, _ in inputs
        ],
        [out, out],
        [pltpu.HBM((rows, width), F32), pltpu.HBM((rows, width), LOW)],
        mib=16,
    )(idx, *[array for array, _ in inputs])


def place_body(plans, idx, mine, came, *outs):
    for out, spans in zip(outs, plans):
        count = sum(high - low for low, high in spans)
        for ref, core in ((mine, idx[0]), (came, 1 - idx[0])):
            at = 0
            for low, high in spans:
                where = pl.ds(pl.multiple_of(core * count + at, 128), high - low)
                out[:, where] = ref[:, low:high].astype(F32)
                at += high - low


def place_columns(idx, mine, came, plans):
    rows = mine.shape[0]
    counts = [2 * sum(high - low for low, high in spans) for spans in plans]
    return call(
        functools.partial(place_body, plans),
        "place_columns",
        (1,),
        [whole(mine), whole(came)],
        [pl.BlockSpec((rows, count), lambda i, s: (0, 0)) for count in counts],
        [shape(rows, count, F32) for count in counts],
        mib=16,
    )(idx, mine, came)


class Halving:
    def __init__(self, sources, half):
        self.sources = sources
        self.half = half
        self.terms = []
        self.last = None

    def start(self, send, link):
        self.terms.append(swap(send, link))

    def layout(self):
        inputs, spans, width = [], [], 0
        for source in self.sources:
            if isinstance(source, Halving):
                more, parts, count = source.layout()
            else:
                count = source.shape[2]
                more, parts = [(in_hbm(source), 0)], [(0, count)]
            inputs += [(array, at + width) for array, at in more]
            spans += [(low + width, high + width) for low, high in parts]
            width += count
        inputs += [(term, 0) for term in self.terms]
        return inputs, spans, width

    def hold(self, *after):
        source = self.sources[0]
        if isinstance(source, Halving):
            source.hold(*after)
        else:
            self.sources[0] = tie(source, *after)

    def step(self, link, *after, first=None):
        if after:
            self.hold(*after)
        self.half //= 2
        inputs, spans, _ = self.layout()
        self.last = sum_slots(inputs, spans, self.half)
        self.terms.append(swap(self.last, link))
        if first is not None:
            first = first + tie(swap(first, link), self.terms[-1])
        return first

    def done(self, idx, *after):
        if after:
            self.hold(*after)
        inputs, spans, _ = self.layout()
        mine, send = last_sum(idx, inputs, spans)
        self.last = mine
        return mine, swap_core(send)


def local(
    hidden,
    segments,
    cotangent,
    in_weight,
    out_weight,
    gate_weight,
    up_weight,
    down_weight,
    conv_weight,
    norm_mix,
    norm_ffn,
):
    groups, block, width = hidden.shape
    rows = groups * block
    size = lax.axis_size("seq")
    seq_index = lax.axis_index("seq")
    core = seq_index % 2
    chip = seq_index // 2
    pair = lax.axis_index("wshard")
    first_core = core == 0
    chips = size // 2
    links = [1 << bit for bit in range(chips.bit_length() - 1)]
    turned = [links[1], links[0]] + links[2:]
    half = out_weight.shape[0] // 2
    cols = 2 * half
    place = chip & 3
    idx = jnp.stack([core, place, pair]).astype(jnp.int32)

    def slots_of(*orders):
        masks = [mask for order in orders for mask in slot_masks(order)]
        return (chip ^ jnp.array(masks, jnp.int32)).astype(jnp.int32)

    weights = (gate_weight, up_weight, down_weight)

    def ordered(flag, mine, other, axis):
        return jnp.where(
            flag,
            jnp.concatenate([mine, other], axis=axis),
            jnp.concatenate([other, mine], axis=axis),
        )

    small = jnp.concatenate([conv_weight, norm_mix[None], norm_ffn[None]], axis=0)
    in_planes = jnp.transpose(in_weight, (1, 0, 2))
    depth = width // 4

    def piece(number):
        from_in = lax.dynamic_slice(in_planes, (0, number * depth, core * half), (3, depth, half))
        from_out = lax.dynamic_slice(out_weight, (core * half, number * depth), (half, depth))
        return jnp.concatenate([from_in.reshape(3 * depth, half), from_out], axis=0)

    sent_zero = piece(place)
    packed = small.reshape(-1, half)
    count = packed.shape[0]
    packed = jnp.pad(packed, ((0, -count % 16), (0, 0)))
    sent_three = jnp.concatenate([piece(place ^ 3), packed], axis=0)
    piece_zero = swap_pair(sent_zero)
    piece_three = swap_pair(sent_three)
    small_other = piece_three[4 * depth : 4 * depth + count].reshape(small.shape)
    hidden, segments = lax.optimization_barrier((hidden, segments, sent_zero))[:2]
    own = hidden.reshape(rows, width)
    other = swap_core(own)
    cot = cotangent.reshape(rows, width)
    cot_far = swap_pair(jnp.concatenate([tie(cot, piece_zero), cot[:16]], axis=0))

    seg_low = segments.astype(LOW)
    seg_other = swap_core(seg_low)

    def with_seg(values, segs):
        return jnp.concatenate(
            [values, jnp.broadcast_to(segs[:, :, None], (groups, segs.shape[1], 128))], axis=2
        )

    def ends(values, segs):
        both = values.reshape(groups, block, width)
        return (
            with_seg(both[:, :2], segs[:, :2]),
            with_seg(both[:, block - 2 :], segs[:, block - 2 :]),
        )

    head, last = ends(own, seg_low)
    other_head, other_last = ends(other, seg_other)
    odd = range(1, size - 1, 2)
    even = range(2, size, 2)
    from_before = jnp.where(
        first_core,
        over_seq(last, [(i, i + 1) for i in odd]),
        over_seq(last, [(i, i + 2) for i in odd]),
    )
    from_after = jnp.where(
        first_core,
        over_seq(head, [(i, i - 2) for i in even]),
        over_seq(head, [(i, i - 1) for i in even]),
    )
    piece_one = swap(piece_zero, 1)
    piece_two = swap(piece_zero, 2)
    far_weights = (piece_zero, piece_one, piece_two, piece_three)

    def after_blocks(outside, own_head, near_head):
        return jnp.where(
            first_core, jnp.stack([near_head, outside]), jnp.stack([outside, own_head])
        )

    before = jnp.where(
        first_core, jnp.stack([from_before, last]), jnp.stack([other_last, from_before])
    )
    after = after_blocks(from_after, head, other_head)
    edges = jnp.concatenate([before, after], axis=0)
    edge_rows = edges[..., :width].reshape(8 * groups, width)
    edge_segs = edges[..., width]
    segs = jnp.stack([seg_low, seg_other])
    segs_ext = jnp.concatenate([edge_segs[:2], segs, edge_segs[2:]], axis=2)
    keeps = jnp.stack(
        [(segs_ext[:, :, at : at + block] == segs).astype(F32) for at in (1, 0, 3, 4)], axis=-1
    ).reshape(2 * rows, 4)

    gains = ordered(pair == 0, small[3:], small_other[3:], 1).astype(F32)
    gain_mix, gain_ffn = gains[:1], gains[1:]
    taps = jnp.concatenate(
        [lax.dynamic_slice_in_dim(part[:3], core * half, half, 1) for part in (small, small_other)],
        axis=1,
    ).astype(F32)

    normed_mix, parts, conv_in, conv_out, mixed, mix_own, mix_other, c_edge = conv_forward(
        idx, own, other, edge_rows, in_planes, out_weight, far_weights, gain_mix, taps, keeps, block
    )
    mix_to_own = swap_core(mix_other)
    mix_to_other = swap_core(mix_own)
    own_x, resid_two = second_norm(
        tie(own, cot_far), mix_own, mix_to_own, gain_ffn, True
    )
    far_x = swap_pair(own_x)
    other_x = second_norm(
        tie(other, own_x), mix_other, mix_to_other, gain_ffn, False
    )[0]

    cot_other = swap_core(tie(cot, piece_zero))
    cot_diag = swap_core(tie(cot_far, own_x))
    total = 4 * rows
    act, d_gate, d_up, term_own, term_other, d_own, d_other = feed_forward(
        idx, [own_x, other_x], [cot, cot_other], weights, total, 0, ()
    )
    diag_x = swap_core(tie(far_x, d_own))
    near_d = swap_core(d_other)
    near_term = swap_core(term_other)
    act, d_gate, d_up, term_far, term_diag, d_far, d_diag = feed_forward(
        idx,
        [far_x, diag_x],
        [cot_far, cot_diag],
        weights,
        total,
        2 * rows // TILE,
        (act, d_gate, d_up),
    )
    d_diag_came = swap_core(d_diag)
    cots = [cot, cot_other, cot_far, cot_diag]
    xs = [own_x, other_x, far_x, diag_x]
    both = slots_of(links, turned)
    cut = 128 * ((act.shape[1] // 128 + 1) // 2)
    half_chips = chips // 2

    def halves(grads):
        low_send, low_keep, high_send, high_keep = grads
        return (low_send, high_send), (
            Halving([low_keep], half_chips),
            Halving([high_keep], half_chips),
        )

    def start(sums, sends):
        sums[0].start(sends[0], links[0])
        sums[1].start(sends[1], links[1])

    gate_sends, gate_sums = halves(weight_grads(both, chips, cut, xs, d_gate))
    start(gate_sums, gate_sends)
    sum_far = add_up(tie(d_far, near_d, near_term, gate_sends[0]), d_diag_came)
    home = swap_pair(sum_far)
    term_sum = add_up(term_far, tie(swap_core(term_diag), sum_far))
    term_home = swap_pair(term_sum)
    down = weight_grads(both, chips, cut, cots, tie(act, term_sum), 0, 2)
    rest_sends, rest_sums = halves(weight_grads(both, chips, cut, xs, d_up, 1, 2, down))

    d_resid, d_low, gain_ffn_terms = resid_back(
        d_own,
        near_d,
        home,
        tie(resid_two, rest_sends[0], gate_sums[0].terms[0], gate_sums[1].terms[0]),
        cot,
        gain_ffn,
    )
    d_near = swap_core(d_low)
    d_head = d_low.reshape(groups, block, width)[:, :2]
    d_after = jnp.where(
        first_core,
        over_seq(d_head, [(i, i - 2) for i in even]),
        over_seq(d_head, [(i, i - 1) for i in even]),
    )
    start(rest_sums, [tie(send, d_after) for send in rest_sends])
    gate_sums[0].step(links[1], d_low)
    gate_sums[1].step(links[0], gate_sums[0].last)
    d_edges = after_blocks(
        d_after, d_head, d_near.reshape(groups, block, width)[:, :2]
    ).reshape(4 * groups, width)
    orders = mix_orders(links)
    slots_mix = slots_of(
        *[[0 if link == "pair" else link for link in order] for order in orders]
    )
    d_proj, sums, send_a, keep_a, send_b, keep_b = conv_back(
        idx,
        slots_mix,
        chips,
        tie(d_low, gate_sums[1].last),
        d_near,
        d_edges,
        gain_ffn_terms,
        (normed_mix, parts, conv_in, conv_out, mixed, c_edge),
        out_weight,
        far_weights,
        taps,
        keeps,
        block,
    )
    rest = links[2:]
    sums_x, sums_z = rest_sums
    sums_z.step(links[0], send_a, term_home)
    sums_x.step(links[1], sums_z.last)
    sum_a = Halving([keep_a], chips)
    sum_b = Halving([keep_b], chips)
    sum_a.start(send_a, orders[0][0])
    gate_last = Halving(list(gate_sums), half_chips // 2)
    gate_last.step(rest[0], sums_x.last)
    sum_b.start(tie(send_b, gate_last.last), orders[1][0])
    d_normed_own, d_normed_other, sums = mix_back(
        idx, own, other, tie(d_proj, gate_last.last), in_planes, far_weights, sums
    )
    ffn_last = Halving([sums_x, sums_z], half_chips // 2)
    ffn_last.step(rest[0], d_normed_own)
    sums = sums + swap_core(tie(sums, ffn_last.last))
    sum_a.step(orders[0][1], ffn_last.last, sums)
    sums = sums + tie(swap(sums, links[0]), sum_a.terms[-1])
    at = sum_a.last
    for link in rest[1:]:
        ffn_last.step(link, at)
        gate_last.step(link, ffn_last.last)
        at = gate_last.last
    gate_mine, gate_came = gate_last.done(idx, at)
    d_normed_came = swap_core(tie(d_normed_other, gate_mine))
    sum_b.step(orders[1][1], gate_mine)
    grad_hidden = hidden_back(
        d_normed_own, d_normed_came, own, tie(d_resid, sum_b.last), gain_mix
    )
    sum_a.step(orders[0][2], grad_hidden, sums)
    sums = sums + tie(swap_pair(tie(sums, sum_a.last)), sum_b.terms[-1])
    sum_b.step(orders[1][2], sum_a.last, sums)
    ffn_mine, ffn_came = ffn_last.done(idx, sum_b.last)
    sums = sums + tie(swap(sums, links[1]), sum_b.terms[-1])
    mix_sums = Halving([sum_a, sum_b], chips // 4)
    at = ffn_mine
    for link in orders[0][3:]:
        sums = mix_sums.step(link, at, sums, first=sums)
        at = mix_sums.last
    block_out = add_up(resid_two, term_own, near_term, tie(term_home, at))
    at = block_out
    half_width = norm_mix.shape[0]
    sums = lax.dynamic_slice_in_dim(sums, pair * half_width, half_width, 1)

    units = act.shape[1]
    (out_gate,) = place_columns(
        idx, gate_mine, tie(gate_came, at), (((0, units),),)
    )
    high = units - cut
    first_high = 2 * cut + high
    out_down, out_up = place_columns(
        idx,
        ffn_mine,
        tie(ffn_came, out_gate),
        (
            ((0, cut), (2 * cut, first_high)),
            ((cut, 2 * cut), (first_high, 2 * units)),
        ),
    )
    mix_mine, mix_came = mix_sums.done(idx, out_up)
    out_out, out_b, out_c, out_x = place_columns(
        idx, mix_mine, mix_came, tuple(((j * half, (j + 1) * half),) for j in range(4))
    )
    return (
        block_out.reshape(groups, block, width),
        grad_hidden.reshape(groups, block, width),
        jnp.stack([out_b, out_c, out_x], axis=1),
        out_out.T,
        out_gate,
        out_up,
        out_down.T,
        sums[:3],
        sums[3],
        sums[4],
    )


def solution(mesh):
    return jax.shard_map(
        local,
        mesh=mesh,
        in_specs=(
            P("wshard", "seq", None),
            P("wshard", "seq"),
            P("wshard", "seq", None),
            P(None, None, "wshard"),
            P("wshard", None),
            P(None, "wshard"),
            P(None, "wshard"),
            P("wshard", None),
            P(None, "wshard"),
            P("wshard"),
            P("wshard"),
        ),
        out_specs=(
            P("wshard", "seq", None),
            P("wshard", "seq", None),
            P("seq", None, "wshard"),
            P("wshard", "seq"),
            P("seq", "wshard"),
            P("seq", "wshard"),
            P("wshard", "seq"),
            P(None, "wshard"),
            P("wshard"),
            P("wshard"),
        ),
        check_vma=False,
    )
```

```python
import functools

import jax
import jax.numpy as jnp
from jax import lax
from jax.experimental import pallas as pl
from jax.experimental.pallas import tpu as pltpu
from jax.sharding import PartitionSpec as P

EPS = 1e-05
LOW = jnp.bfloat16
F32 = jnp.float32
TILE = 256
NT = (((1,), (1,)), ((), ()))
TN = (((0,), (0,)), ((), ()))


def over_seq(block, route):
    return lax.ppermute(block, "seq", route)


def swap_seq(block, mask):
    return over_seq(block, [(i, i ^ mask) for i in range(lax.axis_size("seq"))])


def swap_core(block):
    return swap_seq(block, 1)


def swap_pair(block):
    return lax.ppermute(block, "wshard", [(0, 1), (1, 0)])


def swap(block, link):
    return swap_pair(block) if link == "pair" else swap_seq(block, 2 * link)


def in_hbm(array):
    return pltpu.with_memory_space_constraint(array, pltpu.HBM)


def tie(value, *after):
    return lax.optimization_barrier((value,) + after)[0]


def dot(left, right):
    return jnp.dot(left, right, preferred_element_type=F32)


def dot_nt(left, right):
    return lax.dot_general(left, right, NT, preferred_element_type=F32)


def dot_tn(left, right):
    return lax.dot_general(left, right, TN, preferred_element_type=F32)


def call(
    body, name, grid, in_specs, out_specs, out_shape, scratch=(), scalars=1, aliases=None, mib=36
):
    return pl.pallas_call(
        body,
        grid_spec=pltpu.PrefetchScalarGridSpec(
            num_scalar_prefetch=scalars,
            grid=grid,
            in_specs=in_specs,
            out_specs=out_specs,
            scratch_shapes=list(scratch),
        ),
        out_shape=out_shape,
        input_output_aliases=aliases or {},
        compiler_params=pltpu.CompilerParams(vmem_limit_bytes=mib * 2**20),
        cost_estimate=pl.CostEstimate(flops=1000, bytes_accessed=1000, transcendentals=0),
        name=name,
    )


def shape(rows, cols, kind=LOW):
    return jax.ShapeDtypeStruct((rows, cols), kind)


def whole(array):
    zeros = (0,) * array.ndim
    return pl.BlockSpec(array.shape, lambda *_: zeros)


def normed(values, gain):
    wide = values.astype(F32)
    scale = lax.rsqrt(jnp.mean(wide * wide, axis=-1, keepdims=True) + EPS)
    return wide * scale * gain, scale


def piece_columns(place, j, depth):
    return pl.ds(pl.multiple_of((place ^ j) * depth, depth), depth)


def conv_forward_body(
    block,
    idx,
    own_ref,
    other_ref,
    edge_ref,
    in_ref,
    out_ref,
    r0,
    r1,
    r2,
    r3,
    gain_ref,
    taps_ref,
    keep_ref,
    normed_ref,
    parts_ref,
    conv_in_ref,
    conv_out_ref,
    mixed_ref,
    own_mix_ref,
    other_mix_ref,
    c_edge_ref,
    nx,
    edge_in,
    acc,
):
    step = pl.program_id(0)
    place = idx[1]
    far = (r0, r1, r2, r3)
    half = r0.shape[1]
    depth = r0.shape[0] // 4
    cols = 2 * half
    gain = gain_ref[...]

    def project(load, j):
        mine = dot(load(slice(None)), in_ref[j])
        other = None
        for p in range(4):
            term = dot(load(piece_columns(place, p, depth)), far[p][j * depth : (j + 1) * depth])
            other = term if other is None else other + term
        return jnp.concatenate([mine, other], axis=1)

    @pl.when(step == 0)
    def _():
        count = edge_ref.shape[0]
        nx[:count] = normed(edge_ref[...], gain)[0].astype(LOW)

        def load(columns):
            return nx[:count, columns]

        before = count // 2
        edge_b, edge_c, edge_x = (project(load, j) for j in range(3))
        edge_in[...] = (edge_b[:before] * edge_x[:before]).astype(LOW).astype(F32)
        c_edge_ref[...] = edge_c[before:]

    count = pl.num_programs(0) // 2
    x = jnp.where(step < count, own_ref[...], other_ref[...])
    nx[...] = normed(x, gain)[0].astype(LOW)
    normed_ref[...] = nx[...]

    def load(columns):
        return nx[:, columns]

    b_part, c_part, x_part = (project(load, j) for j in range(3))
    parts_ref[:, :cols] = b_part.astype(LOW)
    parts_ref[:, cols : 2 * cols] = c_part.astype(LOW)
    parts_ref[:, 2 * cols :] = x_part.astype(LOW)
    low_in = (b_part * x_part).astype(LOW)
    conv_in_ref[...] = low_in
    conv_in = low_in.astype(F32)
    groups = own_ref.shape[0] // block
    row = lax.broadcasted_iota(jnp.int32, (block, cols), 0)
    for g in range(groups):
        span = slice(g * block, (g + 1) * block)
        here = conv_in[span]
        base = step * 2 * groups + 2 * g
        two_before = edge_in[pl.ds(base, 1), :]
        one_before = edge_in[pl.ds(base + 1, 1), :]
        lag_one = jnp.where(row == 0, one_before, pltpu.roll(here, 1, 0))
        lag_two = jnp.where(
            row == 0, two_before, jnp.where(row == 1, one_before, pltpu.roll(here, 2, 0))
        )
        conv_out = (
            taps_ref[2:3, :] * here
            + taps_ref[1:2, :] * (keep_ref[span, 0:1] * lag_one)
            + taps_ref[0:1, :] * (keep_ref[span, 1:2] * lag_two)
        )
        conv_out_ref[span, :] = conv_out.astype(LOW)
        mixed_ref[span, :] = (c_part[span] * conv_out).astype(LOW)
    mixed = mixed_ref[...]
    acc[...] = dot(mixed[:, :half], out_ref[...])
    for p in range(4):
        where = piece_columns(place, p, depth)
        acc[:, where] += dot(mixed[:, half:], far[p][3 * depth : 4 * depth])
    mix = acc[...].astype(LOW)

    @pl.when(step < count)
    def _():
        own_mix_ref[...] = mix

    @pl.when(step >= count)
    def _():
        other_mix_ref[...] = mix


def conv_forward(idx, own, other, edges, in_weight, out_weight, far, gain, taps, keeps, block):
    total, width = 2 * own.shape[0], own.shape[1]
    rows = TILE
    half = far[0].shape[1]
    cols = 2 * half

    def rowed(columns):
        return pl.BlockSpec((rows, columns), lambda i, s: (i, 0))

    before = edges.shape[0] // 2
    count = total // rows // 2
    return call(
        functools.partial(conv_forward_body, block),
        "conv_forward",
        (total // rows,),
        [
            pl.BlockSpec((rows, width), lambda i, s: (jnp.minimum(i, count - 1), 0)),
            pl.BlockSpec((rows, width), lambda i, s: (jnp.maximum(i - count, 0), 0)),
            whole(edges),
            pl.BlockSpec((3, width, half), lambda i, s: (0, 0, s[0])),
            pl.BlockSpec((half, width), lambda i, s: (s[0], 0)),
            *[whole(piece) for piece in far],
            whole(gain),
            whole(taps),
            rowed(keeps.shape[1]),
        ],
        [
            rowed(width),
            rowed(3 * cols),
            rowed(cols),
            rowed(cols),
            rowed(cols),
            pl.BlockSpec((rows, width), lambda i, s: (jnp.minimum(i, count - 1), 0)),
            pl.BlockSpec((rows, width), lambda i, s: (jnp.maximum(i - count, 0), 0)),
            pl.BlockSpec((before, cols), lambda i, s: (0, 0)),
        ],
        [
            pltpu.HBM((total, width), LOW),
            pltpu.HBM((total, 3 * cols), LOW),
            pltpu.HBM((total, cols), LOW),
            pltpu.HBM((total, cols), LOW),
            pltpu.HBM((total, cols), LOW),
            shape(total // 2, width),
            shape(total // 2, width),
            shape(before, cols, F32),
        ],
        [
            pltpu.VMEM((rows, width), LOW),
            pltpu.VMEM((before, cols), F32),
            pltpu.VMEM((rows, width), F32),
        ],
    )(idx, own, other, edges, in_hbm(in_weight), in_hbm(out_weight), *far, gain, taps, keeps)


def second_norm_body(x_ref, mine_ref, came_ref, gain_ref, low_ref, *resid_ref):
    two = x_ref[...].astype(F32) + (mine_ref[...].astype(F32) + came_ref[...].astype(F32))
    low_ref[...] = normed(two, gain_ref[...])[0].astype(LOW)
    for ref in resid_ref:
        ref[...] = two


def second_norm(x, mine, came, gain, keep):
    rows, width = mine.shape
    tile = rows // 4

    plain = pl.BlockSpec((tile, width), lambda i: (i, 0))

    return call(
        second_norm_body,
        "second_norm",
        (4,),
        [plain] * 3 + [whole(gain)],
        [plain] * (1 + keep),
        [pltpu.HBM((rows, width), LOW), pltpu.HBM((rows, width), F32)][: 1 + keep],
        scalars=0,
        mib=12,
    )(x, mine, came, gain)


def feed_forward_body(count, held, idx, *refs):
    x_refs, ct_refs = refs[:2], refs[2:4]
    gate_ref, up_ref, down_ref = refs[4:7]
    refs = refs[7 + held :]
    act_ref, d_gate_ref, d_up_ref, term_a, term_b, d_a, d_b = refs
    step = pl.program_id(0)
    first = step < count
    x = jnp.where(first, x_refs[0][...], x_refs[1][...])
    upstream = jnp.where(first, ct_refs[0][...], ct_refs[1][...])
    gate = dot(x, gate_ref[...])
    up_value = dot(x, up_ref[...])
    d_act = dot_nt(upstream, down_ref[...])
    sigma = jax.nn.sigmoid(gate)
    silu_gate = gate * sigma
    act = (silu_gate * up_value).astype(LOW)
    d_gate = (d_act * up_value * (sigma * (1.0 + gate * (1.0 - sigma)))).astype(LOW)
    d_up = (d_act * silu_gate).astype(LOW)
    act_ref[...] = act
    d_gate_ref[...] = d_gate
    d_up_ref[...] = d_up
    d_normed = (dot_nt(d_gate, gate_ref[...]) + dot_nt(d_up, up_ref[...])).astype(LOW)
    term = dot(act, down_ref[...]).astype(LOW)

    @pl.when(first)
    def _():
        d_a[...] = d_normed
        term_a[...] = term

    @pl.when(step >= count)
    def _():
        d_b[...] = d_normed
        term_b[...] = term


def feed_forward(idx, xs, cts, weights, total, start, held):
    gate, up, down = weights
    rows, width = xs[0].shape
    units = gate.shape[1] // 2
    count = rows // TILE

    def rowed(index):
        return pl.BlockSpec((TILE, width), index)

    def lower(i, s):
        return (jnp.minimum(i, count - 1), 0)

    def upper(i, s):
        return (jnp.maximum(i - count, 0), 0)

    any_spec = pl.BlockSpec(memory_space=pl.ANY)
    unit_spec = pl.BlockSpec((TILE, units), lambda i, s: (i + start, 0))
    columns = pl.BlockSpec((width, units), lambda i, s: (0, s[0]))
    return call(
        functools.partial(feed_forward_body, count, len(held)),
        "feed_forward",
        (2 * count,),
        [rowed(lower), rowed(upper)] * 2
        + [columns, columns, pl.BlockSpec((units, width), lambda i, s: (s[0], 0))]
        + [any_spec] * len(held),
        [unit_spec] * 3 + [rowed(lower), rowed(upper)] * 2,
        [pltpu.VMEM((total, units), LOW)] * 3 + [shape(rows, width)] * 4,
        aliases={8 + k: k for k in range(len(held))},
        mib=30,
    )(idx, *[in_hbm(x) for x in (*xs, *cts)], gate, up, down, *held)


def slot_masks(order):
    masks = [0]
    for link in reversed(order):
        masks = masks + [mask ^ link for mask in masks]
    return masks


def grads_body(pieces, cut, chips, part, held, slots, *refs):
    x_hbm, refs = refs[:pieces], refs[pieces:]
    y_hbm, refs = refs[0], refs[1 + held :]
    outs, refs = refs[:4], refs[4:]
    x_buf, y_buf, acc, low_buf, high_buf, x_sems, y_sems, out_sems = refs
    depth = x_buf.shape[1]
    copies = []
    for k in range(pieces):
        from_y = y_hbm.at[pl.ds(k * depth, depth)]
        copies.append(
            pltpu.make_async_copy(x_hbm[k].at[pl.ds(0, depth)], x_buf.at[k], x_sems.at[k])
        )
        copies.append(pltpu.make_async_copy(from_y, y_buf.at[k], y_sems.at[k]))
    for copy in copies:
        copy.start()
    for copy in copies:
        copy.wait()
    for k in range(pieces):
        term = dot_tn(x_buf[k], y_buf[k])
        if k == 0:
            acc[...] = term
        else:
            acc[...] += term
    rows = acc.shape[0] // chips
    half = chips // 2
    copies = []
    for a, (buf, columns) in enumerate(
        ((low_buf, slice(0, cut)), (high_buf, slice(cut, acc.shape[1])))
    ):
        for slot in range(chips):
            where = pl.ds(pl.multiple_of(slots[a * chips + slot] * rows, rows), rows)
            buf[slot] = acc[where, columns].astype(LOW)
        count = buf.shape[2]
        for at, start in enumerate((half, 0)):
            copies.append(
                pltpu.make_async_copy(
                    buf.at[pl.ds(start, half)],
                    outs[2 * a + at].at[:, :, pl.ds(part * count, count)],
                    out_sems.at[a, at],
                )
            )
            copies[-1].start()
    for copy in copies:
        copy.wait()


def weight_grads(slots, chips, cut, xs, y, part=0, parts=1, held=()):
    depth, width = xs[0].shape
    units = y.shape[1]
    pieces = len(xs)
    rows = width // chips
    any_spec = pl.BlockSpec(memory_space=pl.ANY)
    counts = (cut, cut, units - cut, units - cut)
    return call(
        functools.partial(grads_body, pieces, cut, chips, part, len(held)),
        "weight_grads",
        (),
        [any_spec] * (pieces + 1 + len(held)),
        [any_spec] * 4,
        [pltpu.HBM((chips // 2, rows, parts * count), LOW) for count in counts],
        [
            pltpu.VMEM((pieces, depth, width), LOW),
            pltpu.VMEM((pieces, depth, units), LOW),
            pltpu.VMEM((width, units), F32),
            pltpu.VMEM((chips, rows, cut), LOW),
            pltpu.VMEM((chips, rows, units - cut), LOW),
            pltpu.SemaphoreType.DMA((pieces,)),
            pltpu.SemaphoreType.DMA((pieces,)),
            pltpu.SemaphoreType.DMA((2, 2)),
        ],
        aliases={2 + pieces + k: k for k in range(len(held))},
        mib=26,
    )(slots, *[in_hbm(x) for x in xs], y, *held)


def norm_back(upstream, values, scale, gain):
    scaled = values * scale
    weighted = upstream * gain
    inner = jnp.mean(weighted * scaled, axis=-1, keepdims=True)
    return scale * (weighted - scaled * inner), upstream * scaled


def resid_back_body(mine_ref, near_ref, far_ref, two_ref, cot_ref, gain_ref, d_ref, low_ref, sum_ref):
    step = pl.program_id(0)
    upstream = mine_ref[...].astype(F32) + near_ref[...].astype(F32) + far_ref[...].astype(F32)
    two = two_ref[...]
    scale = lax.rsqrt(jnp.mean(two * two, axis=-1, keepdims=True) + EPS)
    back, terms = norm_back(upstream, two, scale, gain_ref[...])
    d_resid = cot_ref[...].astype(F32) + back
    d_ref[...] = d_resid
    low_ref[...] = d_resid.astype(LOW)
    part = jnp.sum(terms.reshape(-1, 8, terms.shape[1]), axis=0)

    @pl.when(step == 0)
    def _():
        sum_ref[...] = part

    @pl.when(step > 0)
    def _():
        sum_ref[...] += part


def resid_back(mine, near, far, two, cot, gain):
    rows, width = two.shape

    def plain(kind=None):
        return pl.BlockSpec((TILE, width), lambda i: (i, 0))

    return call(
        resid_back_body,
        "resid_back",
        (rows // TILE,),
        [plain()] * 5 + [whole(gain)],
        [plain(), plain(), pl.BlockSpec((8, width), lambda i: (0, 0))],
        [pltpu.HBM((rows, width), F32), pltpu.HBM((rows, width), LOW), shape(8, width, F32)],
        scalars=0,
        mib=16,
    )(mine, near, far, two, cot, gain)


def conv_back_body(
    block,
    count,
    chips,
    idx,
    slots,
    own_ref,
    other_ref,
    edge_ref,
    gain_terms_ref,
    normed_ref,
    mixed_ref,
    parts_ref,
    conv_in_ref,
    conv_out_ref,
    c_edge_ref,
    out_ref,
    r0,
    r1,
    r2,
    r3,
    taps_ref,
    keep_ref,
    d_proj,
    sums_ref,
    send_a,
    keep_a,
    send_b,
    keep_b,
    held,
    edge_d,
    in_acc,
    out_acc,
    taps_acc,
    bufs,
    sems,
):
    step = pl.program_id(0)
    place = idx[1]
    far = (r0, r1, r2, r3)
    half = r0.shape[1]
    depth = r0.shape[0] // 4
    cols = 2 * half

    def back_out(load):
        mine = dot_nt(load(slice(None)), out_ref[...])
        other = None
        for p in range(4):
            term = dot_nt(load(piece_columns(place, p, depth)), far[p][3 * depth : 4 * depth])
            other = term if other is None else other + term
        return jnp.concatenate([mine, other], axis=1)

    @pl.when(step == 0)
    def _():
        edge_d[...] = back_out(lambda columns: edge_ref[:, columns]) * c_edge_ref[...]
        in_acc[...] = jnp.zeros_like(in_acc)
        out_acc[...] = jnp.zeros_like(out_acc)
        taps_acc[...] = jnp.zeros_like(taps_acc)

    held[...] = jnp.where(step < count, own_ref[...], other_ref[...])
    d_mixed = back_out(lambda columns: held[:, columns])
    d_conv = d_mixed * parts_ref[:, cols : 2 * cols].astype(F32)
    d_proj[:, cols : 2 * cols] = (d_mixed * conv_out_ref[...].astype(F32)).astype(LOW)
    groups = own_ref.shape[0] // block
    row = lax.broadcasted_iota(jnp.int32, (block, cols), 0)
    for g in range(groups):
        span = slice(g * block, (g + 1) * block)
        here = d_conv[span]
        base = step * 2 * groups + 2 * g
        after_one = edge_d[pl.ds(base, 1), :]
        after_two = edge_d[pl.ds(base + 1, 1), :]
        next_one = jnp.where(row == block - 1, after_one, pltpu.roll(here, block - 1, 0))
        next_two = jnp.where(
            row == block - 1,
            after_two,
            jnp.where(row == block - 2, after_one, pltpu.roll(here, block - 2, 0)),
        )
        next_one = keep_ref[span, 2:3] * next_one
        next_two = keep_ref[span, 3:4] * next_two
        d_in = taps_ref[2:3, :] * here + taps_ref[1:2, :] * next_one + taps_ref[0:1, :] * next_two
        conv_in = conv_in_ref[span, :].astype(F32)
        for k, term in enumerate((next_two, next_one, here)):
            taps_acc[k] += jnp.sum((term * conv_in).reshape(-1, 8, cols), axis=0)
        d_proj[span, :cols] = (d_in * parts_ref[span, 2 * cols :].astype(F32)).astype(LOW)
        d_proj[span, 2 * cols :] = (d_in * parts_ref[span, :cols].astype(F32)).astype(LOW)
    out_acc[...] += dot_tn(held[...], mixed_ref[...])
    in_acc[...] += dot_tn(normed_ref[...], d_proj[...])
    @pl.when(step == 2 * count - 1)
    def _():
        sums_ref[...] = jnp.zeros_like(sums_ref)
        for k in range(3):
            line = jnp.sum(taps_acc[k], axis=0, keepdims=True)
            for part in range(2):
                side = idx[2] if part == 0 else 1 - idx[2]
                at = pl.multiple_of((2 * side + idx[0]) * half, 128)
                sums_ref[k : k + 1, pl.ds(at, half)] = line[:, part * half : (part + 1) * half]
        sums_ref[4:5, :] = jnp.sum(gain_terms_ref[...], axis=0, keepdims=True)
        rows = in_acc.shape[0] // chips
        copies = []
        for a, (halves, keeps, sends) in enumerate(
            (
                (((out_acc, 0), (in_acc, 0)), keep_a, send_a),
                (((in_acc, cols), (in_acc, 2 * cols)), keep_b, send_b),
            )
        ):
            for slot in range(2 * chips):
                number = a * 2 * chips + slot
                where = pl.ds(pl.multiple_of(slots[number] * rows, rows), rows)
                other = slot_pair(a, slot, chips)
                for at, (source, start) in enumerate(halves):
                    low = start + other * half
                    bufs[a, slot, :, at * half : (at + 1) * half] = source[
                        where, low : low + half
                    ].astype(LOW)
            sent = pltpu.make_async_copy(bufs.at[a, pl.ds(chips, chips)], sends, sems.at[a, 0])
            kept = pltpu.make_async_copy(bufs.at[a, pl.ds(0, chips)], keeps, sems.at[a, 1])
            sent.start()
            kept.start()
            copies += [sent, kept]
        for copy in copies:
            copy.wait()


def slot_pair(group, slot, chips):
    return slot // chips if group == 0 else (slot // (chips // 2)) % 2


def mix_orders(links):
    return ["pair"] + links, [links[0], "pair"] + links[1:]


def conv_back(idx, slots, chips, own, other, edges, gain_terms, kept, out_weight, far, taps, keeps, block):
    normed_mix, parts, conv_in, conv_out, mixed, c_edge = kept
    rows, width = own.shape
    half = far[0].shape[1]
    cols = 2 * half
    tile = TILE
    count = rows // tile

    def rowed(columns):
        return pl.BlockSpec((tile, columns), lambda i, s, t: (i, 0))

    def fixed(array):
        zeros = (0,) * array.ndim
        return pl.BlockSpec(array.shape, lambda i, s, t: zeros)

    lower = pl.BlockSpec((tile, width), lambda i, s, t: (jnp.minimum(i, count - 1), 0))
    upper = pl.BlockSpec((tile, width), lambda i, s, t: (jnp.maximum(i - count, 0), 0))
    any_spec = pl.BlockSpec(memory_space=pl.ANY)
    grad = pltpu.HBM((chips, width // chips, cols), LOW)
    return call(
        functools.partial(conv_back_body, block, count, chips),
        "conv_back",
        (2 * count,),
        [
            lower,
            upper,
            fixed(edges),
            fixed(gain_terms),
            rowed(width),
            rowed(cols),
            rowed(3 * cols),
            rowed(cols),
            rowed(cols),
            fixed(c_edge),
            pl.BlockSpec((half, width), lambda i, s, t: (s[0], 0)),
            *[fixed(piece) for piece in far],
            fixed(taps),
            rowed(keeps.shape[1]),
        ],
        [rowed(3 * cols), pl.BlockSpec((8, width), lambda i, s, t: (0, 0))] + [any_spec] * 4,
        [
            pltpu.HBM((2 * rows, 3 * cols), LOW),
            shape(8, width, F32),
        ]
        + [grad] * 4,
        [
            pltpu.VMEM((tile, width), LOW),
            pltpu.VMEM((edges.shape[0], cols), F32),
            pltpu.VMEM((width, 3 * cols), F32),
            pltpu.VMEM((width, cols), F32),
            pltpu.VMEM((3, 8, cols), F32),
            pltpu.VMEM((2, 2 * chips, width // chips, cols), LOW),
            pltpu.SemaphoreType.DMA((2, 2)),
        ],
        scalars=2,
        mib=48,
    )(
        idx,
        slots,
        in_hbm(own),
        in_hbm(other),
        edges,
        gain_terms,
        in_hbm(normed_mix),
        in_hbm(mixed),
        in_hbm(parts),
        in_hbm(conv_in),
        in_hbm(conv_out),
        c_edge,
        in_hbm(out_weight),
        *far,
        taps,
        keeps,
    )


def mix_back_body(count, idx, own_x_ref, other_x_ref, d_proj, in_ref, r0, r1, r2, r3, start_ref, own_ref, other_ref, sums_ref, acc, gain_acc):
    step = pl.program_id(0)
    place = idx[1]
    far = (r0, r1, r2, r3)
    half = r0.shape[1]
    depth = r0.shape[0] // 4
    cols = 2 * half

    @pl.when(step == 0)
    def _():
        gain_acc[...] = jnp.zeros_like(gain_acc)

    total = None
    for j in range(3):
        term = dot_nt(d_proj[:, j * cols : j * cols + half], in_ref[j])
        total = term if total is None else total + term
    acc[...] = total
    for p in range(4):
        where = piece_columns(place, p, depth)
        total = None
        for j in range(3):
            term = dot_nt(d_proj[:, j * cols + half : (j + 1) * cols], far[p][j * depth : (j + 1) * depth])
            total = term if total is None else total + term
        acc[:, where] += total
    wide = jnp.where(step < count, own_x_ref[...], other_x_ref[...]).astype(F32)
    scale = lax.rsqrt(jnp.mean(wide * wide, axis=-1, keepdims=True) + EPS)
    terms = acc[...] * (wide * scale)
    gain_acc[...] += jnp.sum(terms.reshape(-1, 8, terms.shape[1]), axis=0)

    @pl.when(step < count)
    def _():
        own_ref[...] = acc[...].astype(LOW)

    @pl.when(step >= count)
    def _():
        other_ref[...] = acc[...].astype(LOW)

    @pl.when(step == 2 * count - 1)
    def _():
        sums_ref[...] = start_ref[...]
        sums_ref[3:4, :] = jnp.sum(gain_acc[...], axis=0, keepdims=True)


def mix_back(idx, own, other, d_proj, in_weight, far, start):
    total, width = 2 * own.shape[0], own.shape[1]
    half = far[0].shape[1]
    count = total // TILE // 2

    def rowed(columns):
        return pl.BlockSpec((TILE, columns), lambda i, s: (i, 0))

    return call(
        functools.partial(mix_back_body, count),
        "mix_back",
        (2 * count,),
        [
            pl.BlockSpec((TILE, width), lambda i, s: (jnp.minimum(i, count - 1), 0)),
            pl.BlockSpec((TILE, width), lambda i, s: (jnp.maximum(i - count, 0), 0)),
            rowed(d_proj.shape[1]),
            pl.BlockSpec((3, width, half), lambda i, s: (0, 0, s[0])),
            *[whole(piece) for piece in far],
            whole(start),
        ],
        [
            pl.BlockSpec((TILE, width), lambda i, s: (jnp.minimum(i, count - 1), 0)),
            pl.BlockSpec((TILE, width), lambda i, s: (jnp.maximum(i - count, 0), 0)),
            pl.BlockSpec((8, width), lambda i, s: (0, 0)),
        ],
        [shape(total // 2, width), shape(total // 2, width), shape(8, width, F32)],
        [pltpu.VMEM((TILE, width), F32), pltpu.VMEM((8, width), F32)],
    )(idx, own, other, d_proj, in_hbm(in_weight), *far, start)


def hidden_back_body(mine_ref, came_ref, x_ref, d_ref, gain_ref, out_ref):
    upstream = mine_ref[...].astype(F32) + came_ref[...].astype(F32)
    resid = x_ref[...].astype(F32)
    scale = lax.rsqrt(jnp.mean(resid * resid, axis=-1, keepdims=True) + EPS)
    out_ref[...] = d_ref[...] + norm_back(upstream, resid, scale, gain_ref[...])[0]


def hidden_back(mine, came, x, d_resid, gain):
    rows, width = x.shape
    plain = pl.BlockSpec((TILE // 2, width), lambda i: (i, 0))
    return call(
        hidden_back_body,
        "hidden_back",
        (2 * rows // TILE,),
        [plain] * 4 + [whole(gain)],
        plain,
        shape(rows, width, F32),
        scalars=0,
        mib=12,
    )(mine, came, x, d_resid, gain)


def add_up_body(*refs):
    total = refs[0][...].astype(F32)
    for ref in refs[1:-1]:
        total = total + ref[...].astype(F32)
    refs[-1][...] = total.astype(LOW)


def add_up(*arrays):
    rows, width = arrays[0].shape
    tile = TILE // 2
    plain = pl.BlockSpec((tile, width), lambda i: (i, 0))
    return call(
        add_up_body,
        "add_up",
        (rows // tile,),
        [plain] * len(arrays),
        plain,
        pltpu.HBM((rows, width), LOW),
        scalars=0,
        mib=12,
    )(*arrays)


def sum_slots_body(offsets, spans, *refs):
    ins, out = refs[: len(offsets)], refs[len(offsets)]
    for low, high in spans:
        total = None
        for ref, at in zip(ins, offsets):
            if at <= low and high <= at + ref.shape[2]:
                term = ref[:, :, low - at : high - at].astype(F32)
                total = term if total is None else total + term
        out[:, :, low:high] = total.astype(out.dtype)


def sum_slots(inputs, spans, half):
    rows = inputs[0][0].shape[1]
    width = spans[-1][1]
    tile = max(rows // 2, 16)
    return call(
        functools.partial(sum_slots_body, [at for _, at in inputs], spans),
        "sum_slots",
        (rows // tile,),
        [
            pl.BlockSpec((half, tile, array.shape[2]), lambda i: (1, i, 0))
            for array, _ in inputs
        ],
        pl.BlockSpec((half, tile, width), lambda i: (0, i, 0)),
        pltpu.HBM((half, rows, width), LOW),
        scalars=0,
        mib=16,
    )(*[array for array, _ in inputs])


def last_sum_body(offsets, spans, idx, *refs):
    ins, (mine, send) = refs[: len(offsets)], refs[len(offsets) :]
    step = pl.program_id(0)
    for low, high in spans:
        total = None
        for ref, at in zip(ins, offsets):
            if at <= low and high <= at + ref.shape[2]:
                term = ref[0, :, low - at : high - at].astype(F32)
                total = term if total is None else total + term

        @pl.when(step == 0)
        def _():
            mine[:, low:high] = total

        @pl.when(step == 1)
        def _():
            send[:, low:high] = total.astype(LOW)


def last_sum(idx, inputs, spans):
    rows = inputs[0][0].shape[1] // 2
    width = spans[-1][1]
    out = pl.BlockSpec((rows, width), lambda i, s: (0, 0))
    return call(
        functools.partial(last_sum_body, [at for _, at in inputs], spans),
        "last_sum",
        (2,),
        [
            pl.BlockSpec((1, rows, array.shape[2]), lambda i, s: (0, (i + s[0]) % 2, 0))
            for array, _ in inputs
        ],
        [out, out],
        [pltpu.HBM((rows, width), F32), pltpu.HBM((rows, width), LOW)],
        mib=16,
    )(idx, *[array for array, _ in inputs])


def place_body(plans, idx, mine, came, *outs):
    for out, spans in zip(outs, plans):
        count = sum(high - low for low, high in spans)
        for ref, core in ((mine, idx[0]), (came, 1 - idx[0])):
            at = 0
            for low, high in spans:
                where = pl.ds(pl.multiple_of(core * count + at, 128), high - low)
                out[:, where] = ref[:, low:high].astype(F32)
                at += high - low


def place_columns(idx, mine, came, plans):
    rows = mine.shape[0]
    counts = [2 * sum(high - low for low, high in spans) for spans in plans]
    return call(
        functools.partial(place_body, plans),
        "place_columns",
        (1,),
        [whole(mine), whole(came)],
        [pl.BlockSpec((rows, count), lambda i, s: (0, 0)) for count in counts],
        [shape(rows, count, F32) for count in counts],
        mib=16,
    )(idx, mine, came)


def touch_body(steps, start_ref, out, line, sems):
    line[...] = start_ref[...]
    copies = []
    for step in range(steps):
        to = out.at[pl.ds(step * 1024, 16)]
        copies.append(pltpu.make_async_copy(line, to, sems.at[step]))
        copies[-1].start()
    for copy in copies:
        copy.wait()


def touch(start, steps):
    return call(
        functools.partial(touch_body, steps),
        "touch",
        (),
        [pl.BlockSpec(memory_space=pltpu.VMEM)],
        pl.BlockSpec(memory_space=pl.ANY),
        pltpu.HBM((steps * 1024, start.shape[1]), LOW),
        [pltpu.VMEM(start.shape, LOW), pltpu.SemaphoreType.DMA((steps,))],
        scalars=0,
        mib=8,
    )(start)


class Halving:
    def __init__(self, sources, half):
        self.sources = sources
        self.half = half
        self.terms = []
        self.last = None

    def start(self, send, link):
        self.terms.append(swap(send, link))

    def layout(self):
        inputs, spans, width = [], [], 0
        for source in self.sources:
            if isinstance(source, Halving):
                more, parts, count = source.layout()
            else:
                count = source.shape[2]
                more, parts = [(in_hbm(source), 0)], [(0, count)]
            inputs += [(array, at + width) for array, at in more]
            spans += [(low + width, high + width) for low, high in parts]
            width += count
        inputs += [(term, 0) for term in self.terms]
        return inputs, spans, width

    def hold(self, *after):
        source = self.sources[0]
        if isinstance(source, Halving):
            source.hold(*after)
        else:
            self.sources[0] = tie(source, *after)

    def step(self, link, *after, first=None):
        if after:
            self.hold(*after)
        self.half //= 2
        inputs, spans, _ = self.layout()
        self.last = sum_slots(inputs, spans, self.half)
        self.terms.append(swap(self.last, link))
        if first is not None:
            first = first + tie(swap(first, link), self.terms[-1])
        return first

    def done(self, idx, *after):
        if after:
            self.hold(*after)
        inputs, spans, _ = self.layout()
        mine, send = last_sum(idx, inputs, spans)
        self.last = mine
        return mine, swap_core(send)


def local(
    hidden,
    segments,
    cotangent,
    in_weight,
    out_weight,
    gate_weight,
    up_weight,
    down_weight,
    conv_weight,
    norm_mix,
    norm_ffn,
):
    groups, block, width = hidden.shape
    rows = groups * block
    size = lax.axis_size("seq")
    seq_index = lax.axis_index("seq")
    core = seq_index % 2
    chip = seq_index // 2
    pair = lax.axis_index("wshard")
    first_core = core == 0
    chips = size // 2
    links = [1 << bit for bit in range(chips.bit_length() - 1)]
    turned = [links[1], links[0]] + links[2:]
    half = out_weight.shape[0] // 2
    cols = 2 * half
    place = chip & 3
    idx = jnp.stack([core, place, pair]).astype(jnp.int32)

    def slots_of(*orders):
        masks = [mask for order in orders for mask in slot_masks(order)]
        return (chip ^ jnp.array(masks, jnp.int32)).astype(jnp.int32)

    weights = (gate_weight, up_weight, down_weight)

    def ordered(flag, mine, other, axis):
        return jnp.where(
            flag,
            jnp.concatenate([mine, other], axis=axis),
            jnp.concatenate([other, mine], axis=axis),
        )

    small = jnp.concatenate([conv_weight, norm_mix[None], norm_ffn[None]], axis=0)
    in_planes = jnp.transpose(in_weight, (1, 0, 2))
    depth = width // 4

    def piece(number):
        from_in = lax.dynamic_slice(in_planes, (0, number * depth, core * half), (3, depth, half))
        from_out = lax.dynamic_slice(out_weight, (core * half, number * depth), (half, depth))
        return jnp.concatenate([from_in.reshape(3 * depth, half), from_out], axis=0)

    sent_zero = piece(place)
    packed = small.reshape(-1, half)
    count = packed.shape[0]
    packed = jnp.pad(packed, ((0, -count % 16), (0, 0)))
    sent_three = jnp.concatenate([piece(place ^ 3), packed], axis=0)
    piece_zero = swap_pair(sent_zero)
    piece_three = swap_pair(sent_three)
    small_other = piece_three[4 * depth : 4 * depth + count].reshape(small.shape)
    touched = touch(tie(hidden[0, :16], sent_zero), 24)
    hidden, segments = lax.optimization_barrier((hidden, segments, sent_zero))[:2]
    own = hidden.reshape(rows, width)
    other = swap_core(own)
    cot = cotangent.reshape(rows, width)
    cot_far = swap_pair(jnp.concatenate([tie(cot, piece_zero), cot[:16]], axis=0))

    seg_low = segments.astype(LOW)
    seg_other = swap_core(seg_low)

    def with_seg(values, segs):
        return jnp.concatenate(
            [values, jnp.broadcast_to(segs[:, :, None], (groups, segs.shape[1], 128))], axis=2
        )

    def ends(values, segs, first=None):
        both = values.reshape(groups, block, width)
        heads = both[:, :2]
        if first is not None:
            heads = jnp.concatenate([first[None, :2], heads[1:]], axis=0)
        return (
            with_seg(heads, segs[:, :2]),
            with_seg(both[:, block - 2 :], segs[:, block - 2 :]),
        )

    head, last = ends(own, seg_low, touched)
    other_head, other_last = ends(other, seg_other)
    odd = range(1, size - 1, 2)
    even = range(2, size, 2)
    from_before = jnp.where(
        first_core,
        over_seq(last, [(i, i + 1) for i in odd]),
        over_seq(last, [(i, i + 2) for i in odd]),
    )
    from_after = jnp.where(
        first_core,
        over_seq(head, [(i, i - 2) for i in even]),
        over_seq(head, [(i, i - 1) for i in even]),
    )
    piece_one = swap(piece_zero, 1)
    piece_two = swap(piece_zero, 2)
    far_weights = (piece_zero, piece_one, piece_two, piece_three)

    def after_blocks(outside, own_head, near_head):
        return jnp.where(
            first_core, jnp.stack([near_head, outside]), jnp.stack([outside, own_head])
        )

    before = jnp.where(
        first_core, jnp.stack([from_before, last]), jnp.stack([other_last, from_before])
    )
    after = after_blocks(from_after, head, other_head)
    edges = jnp.concatenate([before, after], axis=0)
    edge_rows = edges[..., :width].reshape(8 * groups, width)
    edge_segs = edges[..., width]
    segs = jnp.stack([seg_low, seg_other])
    segs_ext = jnp.concatenate([edge_segs[:2], segs, edge_segs[2:]], axis=2)
    keeps = jnp.stack(
        [(segs_ext[:, :, at : at + block] == segs).astype(F32) for at in (1, 0, 3, 4)], axis=-1
    ).reshape(2 * rows, 4)

    gains = ordered(pair == 0, small[3:], small_other[3:], 1).astype(F32)
    gain_mix, gain_ffn = gains[:1], gains[1:]
    taps = jnp.concatenate(
        [lax.dynamic_slice_in_dim(part[:3], core * half, half, 1) for part in (small, small_other)],
        axis=1,
    ).astype(F32)

    normed_mix, parts, conv_in, conv_out, mixed, mix_own, mix_other, c_edge = conv_forward(
        idx, own, other, edge_rows, in_planes, out_weight, far_weights, gain_mix, taps, keeps, block
    )
    mix_to_own = swap_core(mix_other)
    mix_to_other = swap_core(mix_own)
    own_x, resid_two = second_norm(
        tie(own, cot_far), mix_own, mix_to_own, gain_ffn, True
    )
    far_x = swap_pair(own_x)
    other_x = second_norm(
        tie(other, own_x), mix_other, mix_to_other, gain_ffn, False
    )[0]

    cot_other = swap_core(tie(cot, piece_zero))
    cot_diag = swap_core(tie(cot_far, own_x))
    total = 4 * rows
    act, d_gate, d_up, term_own, term_other, d_own, d_other = feed_forward(
        idx, [own_x, other_x], [cot, cot_other], weights, total, 0, ()
    )
    diag_x = swap_core(tie(far_x, d_own))
    near_d = swap_core(d_other)
    near_term = swap_core(term_other)
    act, d_gate, d_up, term_far, term_diag, d_far, d_diag = feed_forward(
        idx,
        [far_x, diag_x],
        [cot_far, cot_diag],
        weights,
        total,
        2 * rows // TILE,
        (act, d_gate, d_up),
    )
    d_diag_came = swap_core(d_diag)
    cots = [cot, cot_other, cot_far, cot_diag]
    xs = [own_x, other_x, far_x, diag_x]
    both = slots_of(links, turned)
    cut = 128 * ((act.shape[1] // 128 + 1) // 2)
    half_chips = chips // 2

    def halves(grads):
        low_send, low_keep, high_send, high_keep = grads
        return (low_send, high_send), (
            Halving([low_keep], half_chips),
            Halving([high_keep], half_chips),
        )

    def start(sums, sends):
        sums[0].start(sends[0], links[0])
        sums[1].start(sends[1], links[1])

    gate_sends, gate_sums = halves(weight_grads(both, chips, cut, xs, d_gate))
    start(gate_sums, gate_sends)
    sum_far = add_up(tie(d_far, near_d, near_term, gate_sends[0]), d_diag_came)
    home = swap_pair(sum_far)
    term_sum = add_up(term_far, tie(swap_core(term_diag), sum_far))
    term_home = swap_pair(term_sum)
    down = weight_grads(both, chips, cut, cots, tie(act, term_sum), 0, 2)
    rest_sends, rest_sums = halves(weight_grads(both, chips, cut, xs, d_up, 1, 2, down))

    d_resid, d_low, gain_ffn_terms = resid_back(
        d_own,
        near_d,
        home,
        tie(resid_two, rest_sends[0], gate_sums[0].terms[0], gate_sums[1].terms[0]),
        cot,
        gain_ffn,
    )
    d_near = swap_core(d_low)
    d_head = d_low.reshape(groups, block, width)[:, :2]
    d_after = jnp.where(
        first_core,
        over_seq(d_head, [(i, i - 2) for i in even]),
        over_seq(d_head, [(i, i - 1) for i in even]),
    )
    start(rest_sums, [tie(send, d_after) for send in rest_sends])
    gate_sums[0].step(links[1], d_low)
    gate_sums[1].step(links[0], gate_sums[0].last)
    d_edges = after_blocks(
        d_after, d_head, d_near.reshape(groups, block, width)[:, :2]
    ).reshape(4 * groups, width)
    orders = mix_orders(links)
    slots_mix = slots_of(
        *[[0 if link == "pair" else link for link in order] for order in orders]
    )
    d_proj, sums, send_a, keep_a, send_b, keep_b = conv_back(
        idx,
        slots_mix,
        chips,
        tie(d_low, gate_sums[1].last),
        d_near,
        d_edges,
        gain_ffn_terms,
        (normed_mix, parts, conv_in, conv_out, mixed, c_edge),
        out_weight,
        far_weights,
        taps,
        keeps,
        block,
    )
    rest = links[2:]
    sums_x, sums_z = rest_sums
    sums_z.step(links[0], send_a, term_home)
    sums_x.step(links[1], sums_z.last)
    sum_a = Halving([keep_a], chips)
    sum_b = Halving([keep_b], chips)
    sum_a.start(send_a, orders[0][0])
    gate_last = Halving(list(gate_sums), half_chips // 2)
    gate_last.step(rest[0], sums_x.last)
    sum_b.start(tie(send_b, gate_last.last), orders[1][0])
    d_normed_own, d_normed_other, sums = mix_back(
        idx, own, other, tie(d_proj, gate_last.last), in_planes, far_weights, sums
    )
    ffn_last = Halving([sums_x, sums_z], half_chips // 2)
    ffn_last.step(rest[0], d_normed_own)
    sums = sums + swap_core(tie(sums, ffn_last.last))
    sum_a.step(orders[0][1], ffn_last.last, sums)
    sums = sums + tie(swap(sums, links[0]), sum_a.terms[-1])
    at = sum_a.last
    for link in rest[1:]:
        ffn_last.step(link, at)
        gate_last.step(link, ffn_last.last)
        at = gate_last.last
    gate_mine, gate_came = gate_last.done(idx, at)
    d_normed_came = swap_core(tie(d_normed_other, gate_mine))
    sum_b.step(orders[1][1], gate_mine)
    grad_hidden = hidden_back(
        d_normed_own, d_normed_came, own, tie(d_resid, sum_b.last), gain_mix
    )
    sum_a.step(orders[0][2], grad_hidden, sums)
    sums = sums + tie(swap_pair(tie(sums, sum_a.last)), sum_b.terms[-1])
    sum_b.step(orders[1][2], sum_a.last, sums)
    ffn_mine, ffn_came = ffn_last.done(idx, sum_b.last)
    sums = sums + tie(swap(sums, links[1]), sum_b.terms[-1])
    mix_sums = Halving([sum_a, sum_b], chips // 4)
    at = ffn_mine
    for link in orders[0][3:]:
        sums = mix_sums.step(link, at, sums, first=sums)
        at = mix_sums.last
    block_out = add_up(resid_two, term_own, near_term, tie(term_home, at))
    at = block_out
    half_width = norm_mix.shape[0]
    sums = lax.dynamic_slice_in_dim(sums, pair * half_width, half_width, 1)

    units = act.shape[1]
    (out_gate,) = place_columns(
        idx, gate_mine, tie(gate_came, at), (((0, units),),)
    )
    high = units - cut
    first_high = 2 * cut + high
    out_down, out_up = place_columns(
        idx,
        ffn_mine,
        tie(ffn_came, out_gate),
        (
            ((0, cut), (2 * cut, first_high)),
            ((cut, 2 * cut), (first_high, 2 * units)),
        ),
    )
    mix_mine, mix_came = mix_sums.done(idx, out_up)
    out_out, out_b, out_c, out_x = place_columns(
        idx, mix_mine, mix_came, tuple(((j * half, (j + 1) * half),) for j in range(4))
    )
    return (
        block_out.reshape(groups, block, width),
        grad_hidden.reshape(groups, block, width),
        jnp.stack([out_b, out_c, out_x], axis=1),
        out_out.T,
        out_gate,
        out_up,
        out_down.T,
        sums[:3],
        sums[3],
        sums[4],
    )


def solution(mesh):
    return jax.shard_map(
        local,
        mesh=mesh,
        in_specs=(
            P("wshard", "seq", None),
            P("wshard", "seq"),
            P("wshard", "seq", None),
            P(None, None, "wshard"),
            P("wshard", None),
            P(None, "wshard"),
            P(None, "wshard"),
            P("wshard", None),
            P(None, "wshard"),
            P("wshard"),
            P("wshard"),
        ),
        out_specs=(
            P("wshard", "seq", None),
            P("wshard", "seq", None),
            P("seq", None, "wshard"),
            P("wshard", "seq"),
            P("seq", "wshard"),
            P("seq", "wshard"),
            P("wshard", "seq"),
            P(None, "wshard"),
            P("wshard"),
            P("wshard"),
        ),
        check_vma=False,
    )
```
